32 devices in a mesh: ctx: 4 (over y, x), fsdp: 8 (over z, core).
Axes of the slice: x: 2, y: 2, z: 4, core: 2. Of those that a mesh axis runs over, the one named last changes fastest.
Arguments:
- queries: bfloat16 [4096, 2048], P(('ctx', 'fsdp')), may hold values from -8 to 8
- keys: bfloat16 [4096, 1024], P(('ctx', 'fsdp')), may hold values from -8 to 8
- values: bfloat16 [4096, 1024], P(('ctx', 'fsdp')), may hold values from -6 to 6
- grad_out: bfloat16 [4096, 2048], P(('ctx', 'fsdp')), may hold values from -6 to 6
- segment: int32 [4096], P(('ctx', 'fsdp')), may hold values from 0 to 7, never falling along the last dimension, each value on 1 to 2048 neighbouring positions
Outputs:
- grad_queries: bfloat16 [4096, 2048], P(('ctx', 'fsdp'))
- grad_keys: bfloat16 [4096, 1024], P(('ctx', 'fsdp'))
- grad_values: bfloat16 [4096, 1024], P(('ctx', 'fsdp'))
The draws below stay inside these ranges and needn't reach their ends.
Inputs may be any that keep to these rules, and one draw needn't show every extreme that they name: `segment`: document ids never fall along the sequence; every document holds 1 to 2048 tokens and one holds exactly 2048.
All inputs are finite; a program needn't handle non-finite values.
Results may differ from the reference program's by a relative error of at most 0.0071.
Values may be sent and summed in bfloat16 or wider, within the bound.
No kernel may reach another device: no remote copies, remote signals or barrier semaphores. Data moves between devices by JAX's collectives and lax.ppermute only.
A program may use at most 64 MiB of HBM per device.

```python
import math
import jax
import jax.numpy as jnp
import numpy as np
from jax import lax

HEADS = 16
KV_HEADS = 8
HEAD_DIM = 128
WINDOW = 512
TOK_DEV = 128
TOKENS = 4096
DOCS = 8
DOC_MOST = 2048


def block_scale(key, extent, pieces, low, top_value):
    def one(position, shards_of):
        draws = jax.random.uniform(jax.random.fold_in(jax.random.fold_in(key, 6), position), (shards_of,), jnp.float32, low / len(pieces), top_value / len(pieces))
        return jnp.repeat(jnp.exp(draws), extent[position] // shards_of).reshape((-1,) + (1,) * (len(extent) - position - 1))

    gain = one(*pieces[0])
    for cut in pieces[1:]:
        gain = gain * one(*cut)
    return gain


def split_up(amount, total, most, slope):
    portions = [(1 << 20) // math.isqrt(grade ** slope) + 1 for grade in range(2, amount + 1)]
    spare, counts = total - most - (amount - 1), [1] * (amount - 1)
    while spare > 0:
        candidates = [i for i in range(amount - 1) if counts[i] < most]
        whole, left = sum([portions[i] for i in candidates]), spare
        for i in candidates:
            addition = min(most - counts[i], max(1, left * portions[i] // whole), spare)
            counts[i] = counts[i] + addition
            spare = spare - addition
    return np.array([most] + counts)


def ragged_sizes(own_key, count, total, most, slope):
    if count == 2:
        one = jax.random.randint(own_key, (), max(1, total - most), min(most, total - 1) + 1)
        return jnp.stack([one, total - one])
    tallies = jnp.asarray(split_up(count, total, most, slope), jnp.int32)
    pairs = (count - 1) // 2
    donor, sink = tallies[1:1 + 2 * pairs:2], tallies[2:2 + 2 * pairs:2]
    slack = jnp.minimum(donor - 1, most - sink)
    shifted = jax.random.randint(jax.random.fold_in(own_key, 1), (pairs,), 0, 1 << 20) % (slack + 1)
    tallies = tallies.at[1:1 + 2 * pairs:2].set(donor - shifted).at[2:2 + 2 * pairs:2].set(sink + shifted)
    return tallies[jax.random.permutation(jax.random.fold_in(own_key, 2), count)]


def noise(stream_key, shape, scale, limit, shards=(), kind=jnp.bfloat16):
    values = scale * jax.random.normal(stream_key, shape, jnp.float32)
    if shards:
        values = values * block_scale(stream_key, shape, shards, -0.22, 0.18)
    return jnp.clip(values, -limit, limit).astype(kind)


def setup_inputs(seed: int = 0) -> dict:
    key_list = jax.random.split(jax.random.key(seed), 6)
    return {
        "queries": noise(key_list[0], (TOKENS, HEADS * HEAD_DIM), 2.0, 8.0, ((0, 32),)),
        "keys": noise(key_list[1], (TOKENS, KV_HEADS * HEAD_DIM), 2.0, 8.0, ((0, 32),)),
        "values": noise(key_list[2], (TOKENS, KV_HEADS * HEAD_DIM), 1.0, 6.0, ((0, 32),)),
        "grad_out": noise(key_list[3], (TOKENS, HEADS * HEAD_DIM), 1.0, 6.0, ((0, 32),)),
        "segment": jnp.searchsorted(jnp.cumsum(ragged_sizes(key_list[4], DOCS, TOKENS, DOC_MOST, 2)), jnp.arange(TOKENS), side="right").astype(jnp.int32),
    }


softcap = 50.0
inv_scale = 1.0 / 12.0


def tile_grads(query_rows, key_rows, value_rows, grad_rows, visible):
    raw_scores = jnp.einsum('ngrd,mgd->grnm', query_rows, key_rows)
    capped = softcap * jnp.tanh(raw_scores * inv_scale / softcap)
    weights = jnp.where(visible[None, None], jnp.exp(capped), jnp.float32(0.0))
    totals = jnp.sum(weights, axis=-1, keepdims=True)
    probs = weights / totals
    probs_low = lax.optimization_barrier(probs.astype(jnp.bfloat16)).astype(jnp.float32)
    attended = jnp.einsum('grnm,mgd->ngrd', probs_low, value_rows)
    row_terms = jnp.transpose(jnp.sum(grad_rows * attended, axis=-1), (1, 2, 0))[..., None]
    dprobs = jnp.einsum('ngrd,mgd->grnm', grad_rows, value_rows)
    dscore = probs * (dprobs - row_terms) * (1.0 - (capped / softcap) ** 2) * inv_scale
    dscore_low = lax.optimization_barrier(dscore.astype(jnp.bfloat16)).astype(jnp.float32)
    grad_q = jnp.einsum('grnm,mgd->ngrd', dscore_low, key_rows)
    grad_k = jnp.einsum('grnm,ngrd->mgd', dscore_low, query_rows)
    grad_v = jnp.einsum('grnm,ngrd->mgd', probs_low, grad_rows)
    return grad_q, grad_k, grad_v


def reference(queries, keys, values, grad_out, segment):
    reach = (WINDOW + TOK_DEV - 1) // TOK_DEV
    padding = reach * TOK_DEV
    group_size = HEADS // KV_HEADS
    kv_width = KV_HEADS * HEAD_DIM
    block_count = TOKENS // TOK_DEV
    keys_pad = jnp.concatenate([jnp.zeros((padding, kv_width), keys.dtype), keys], 0)
    values_pad = jnp.concatenate([jnp.zeros((padding, kv_width), values.dtype), values], 0)
    segment_pad = jnp.concatenate([-jnp.ones((padding,), jnp.int32), segment.astype(jnp.int32)], 0)
    row_index = jnp.arange(TOK_DEV, dtype=jnp.int32)
    col_index = jnp.arange(padding + TOK_DEV, dtype=jnp.int32)
    offsets = row_index[:, None] + padding - col_index[None, :]

    def advance(carry, block):
        grad_k_acc, grad_v_acc = carry
        start_row = (block * TOK_DEV).astype(jnp.int32)
        query_rows = lax.dynamic_slice_in_dim(queries, start_row, TOK_DEV, 0).astype(jnp.float32)
        query_rows = query_rows.reshape(TOK_DEV, KV_HEADS, group_size, HEAD_DIM)
        grad_rows = lax.dynamic_slice_in_dim(grad_out, start_row, TOK_DEV, 0).astype(jnp.float32)
        grad_rows = grad_rows.reshape(TOK_DEV, KV_HEADS, group_size, HEAD_DIM)
        key_rows = lax.dynamic_slice_in_dim(keys_pad, start_row, padding + TOK_DEV, 0).astype(jnp.float32)
        key_rows = key_rows.reshape(padding + TOK_DEV, KV_HEADS, HEAD_DIM)
        value_rows = lax.dynamic_slice_in_dim(values_pad, start_row, padding + TOK_DEV, 0).astype(jnp.float32)
        value_rows = value_rows.reshape(padding + TOK_DEV, KV_HEADS, HEAD_DIM)
        seg_query = lax.dynamic_slice_in_dim(segment, start_row, TOK_DEV, 0)
        seg_key = lax.dynamic_slice_in_dim(segment_pad, start_row, padding + TOK_DEV, 0)
        visible = (seg_query[:, None] == seg_key[None, :]) & (offsets >= 0) & (offsets < WINDOW)
        grad_q, grad_k, grad_v = tile_grads(query_rows, key_rows, value_rows, grad_rows, visible)
        old_k = lax.dynamic_slice_in_dim(grad_k_acc, start_row, padding + TOK_DEV, 0)
        old_v = lax.dynamic_slice_in_dim(grad_v_acc, start_row, padding + TOK_DEV, 0)
        grad_k_acc = lax.dynamic_update_slice_in_dim(grad_k_acc, old_k + grad_k.reshape(-1, kv_width), start_row, 0)
        grad_v_acc = lax.dynamic_update_slice_in_dim(grad_v_acc, old_v + grad_v.reshape(-1, kv_width), start_row, 0)
        return (grad_k_acc, grad_v_acc), grad_q.reshape(TOK_DEV, HEADS * HEAD_DIM).astype(jnp.bfloat16)

    zero_acc = jnp.zeros((TOKENS + padding, kv_width), jnp.float32)
    (grad_k_acc, grad_v_acc), grad_q_blocks = lax.scan(advance, (zero_acc, zero_acc), jnp.arange(block_count, dtype=jnp.int32))
    grad_queries = grad_q_blocks.reshape(TOKENS, HEADS * HEAD_DIM)
    return (grad_queries, grad_k_acc[padding:].astype(jnp.bfloat16), grad_v_acc[padding:].astype(jnp.bfloat16))
```

```python
import functools

import jax
import jax.numpy as jnp
from jax import lax
from jax.experimental import pallas as pl
from jax.experimental.pallas import tpu as pltpu
from jax.sharding import PartitionSpec as P

HEAD_DIM = 128
WINDOW = 512
SOFTCAP = 50.0
SCALE = 1.0 / 12.0
LOG2E = 1.4426950408889634
AXES = ("ctx", "fsdp")
NT = (((1,), (1,)), ((), ()))
NN = (((1,), (0,)), ((), ()))
SEG_ROWS = 16


def dot(a, b, dims):
    return lax.dot_general(a, b, dims, preferred_element_type=jnp.float32)


def swap(x):
    n = lax.axis_size(AXES)
    return lax.ppermute(x, AXES, [(i, i ^ 1) for i in range(n)])


def hop(x, chips):
    n = lax.axis_size(AXES)
    by = 2 * chips
    return lax.ppermute(x, AXES, [(i, i + by) for i in range(n) if 0 <= i + by < n])


def fill_starts(core, lo_ref, sega_ref, segb_ref, lo_s, tok):
    lo = lo_ref[...]
    seg0 = lo[2:3, 0:1].astype(jnp.float32)
    far = jnp.where(sega_ref[0:1, : 2 * tok].astype(jnp.float32) == seg0, 1.0, 0.0)
    far = far + jnp.where(segb_ref[0:1, : 2 * tok].astype(jnp.float32) == seg0, 1.0, 0.0)
    count = jnp.sum(far, axis=1, keepdims=True).astype(jnp.int32)
    row = lax.broadcasted_iota(jnp.int32, (1, tok), 1)
    for r in range(2):
        half = lax.bitwise_xor(core, r)
        mine = lo[r : r + 1]
        mine = jnp.where(mine < 0, WINDOW - count, mine) - half * tok
        mine = jnp.maximum(mine, row + 1)
        lo_s[r, 0:1, :] = jnp.concatenate([mine, mine], 1)


def gather_keys(core, pieces, dst, tok):
    for chip, ref in enumerate(pieces):
        for r in range(2):
            at = 2 * tok * chip + tok * lax.bitwise_xor(core, r)
            dst[pl.ds(pl.multiple_of(at, tok), tok), :] = ref[pl.ds(r * tok, tok), :]


def heads_of(ref):
    return jnp.concatenate([ref[:, :HEAD_DIM], ref[:, HEAD_DIM:]], 0)


def weights_of(key_rows, q_rows, lo, jj, last, tok):
    s = dot(key_rows, q_rows, NT)
    t = jnp.tanh(s * (SCALE / SOFTCAP))
    w = jnp.exp2(t * (SOFTCAP * LOG2E))
    pos = lax.broadcasted_iota(jnp.int32, s.shape, 0)
    ok = pos + jj * tok >= lo
    if last:
        col = lax.broadcasted_iota(jnp.int32, s.shape, 1)
        col = jnp.where(col >= tok, col - tok, col)
        ok = ok & (pos <= col)
    return t, jnp.where(ok, w, 0.0)


def fold(x):
    return jnp.sum(x.reshape(x.shape[0] // 8, 8, x.shape[1]), axis=0)


def value_kernel(tok, core_ref, lo_ref, sega, segb, q0, q1, g0, g1, kb, ka, kc,
                 dvb, dva, dvc, inv_ref, lo_s, k_s, w_s, dv_s):
    core = core_ref[0]
    blocks = WINDOW // tok + 1

    @pl.when(pl.program_id(0) == 0)
    def _():
        fill_starts(core, lo_ref, sega, segb, lo_s, tok)

    gather_keys(core, (kb, ka, kc), k_s, tok)
    dv_s[...] = jnp.zeros_like(dv_s)
    for r, (q, g) in enumerate(((q0, g0), (q1, g1))):
        base = lax.bitwise_xor(core, r) * tok
        q_rows, g_rows = heads_of(q), heads_of(g)
        lo = lo_s[r, 0:1, :]
        total = jnp.zeros((8, 2 * tok), jnp.float32)
        for jj in range(blocks):
            rows = pl.ds(pl.multiple_of(base + jj * tok, tok), tok)
            _, w = weights_of(k_s[rows, :], q_rows, lo, jj, jj == blocks - 1, tok)
            w_s[jj] = w
            total = total + fold(w)
        inv = 1.0 / jnp.sum(total, axis=0, keepdims=True)
        inv_ref[0, r : r + 1, :] = inv
        for jj in range(blocks):
            rows = pl.ds(pl.multiple_of(base + jj * tok, tok), tok)
            low = (w_s[jj] * inv).astype(jnp.bfloat16)
            dv_s[rows, :] += dot(low, g_rows, NN)
    put_back(core, dv_s, (dvb, dva, dvc), tok)


def put_back(core, src, outs, tok):
    for chip, ref in enumerate(outs):
        for r in range(2):
            at = 2 * tok * chip + tok * lax.bitwise_xor(core, r)
            piece = src[pl.ds(pl.multiple_of(at, tok), tok), :]
            ref[pl.ds(r * tok, tok), :] = piece.astype(ref.dtype)


def score_kernel(tok, core_ref, lo_ref, sega, segb, q0, q1, g0, g1, kb, ka, kc, vb, va, vc,
                 inv_ref, dkb, dka, dkc, dq0, dq1, lo_s, k_s, v_s, p_s, t_s, dp_s, dk_s):
    core = core_ref[0]
    blocks = WINDOW // tok + 1

    @pl.when(pl.program_id(0) == 0)
    def _():
        fill_starts(core, lo_ref, sega, segb, lo_s, tok)

    gather_keys(core, (kb, ka, kc), k_s, tok)
    gather_keys(core, (vb, va, vc), v_s, tok)
    dk_s[...] = jnp.zeros_like(dk_s)
    for r, (q, g, dq) in enumerate(((q0, g0, dq0), (q1, g1, dq1))):
        base = lax.bitwise_xor(core, r) * tok
        q_rows, g_rows = heads_of(q), heads_of(g)
        lo = lo_s[r, 0:1, :]
        inv = inv_ref[0, r : r + 1, :]
        term = jnp.zeros((8, 2 * tok), jnp.float32)
        for jj in range(blocks):
            rows = pl.ds(pl.multiple_of(base + jj * tok, tok), tok)
            t, w = weights_of(k_s[rows, :], q_rows, lo, jj, jj == blocks - 1, tok)
            p = w * inv
            dp = dot(v_s[rows, :], g_rows, NT)
            term = term + fold(p.astype(jnp.bfloat16).astype(jnp.float32) * dp)
            p_s[jj] = p * (SCALE - t * t * SCALE)
            dp_s[jj] = dp
        term = jnp.sum(term, axis=0, keepdims=True)
        dq_t = jnp.zeros((HEAD_DIM, 2 * tok), jnp.float32)
        for jj in range(blocks):
            rows = pl.ds(pl.multiple_of(base + jj * tok, tok), tok)
            ds = (p_s[jj] * (dp_s[jj] - term)).astype(jnp.bfloat16)
            dk_s[rows, :] += dot(ds, q_rows, NN)
            dq_t = dq_t + dot(k_s[rows, :].T, ds, NN)
        dq_rows = dq_t.T.astype(jnp.bfloat16)
        dq[:, :HEAD_DIM] = dq_rows[:tok]
        dq[:, HEAD_DIM:] = dq_rows[tok:]
    put_back(core, dk_s, (dkb, dka, dkc), tok)


def local(queries, keys, values, grad_out, segment):
    tok = queries.shape[0]
    kv_width = keys.shape[1]
    half = kv_width // 2
    groups = half // HEAD_DIM
    q_half = queries.shape[1] // 2
    bf16, f32 = jnp.bfloat16, jnp.float32
    core = lax.rem(lax.axis_index(AXES), 2)
    core_arr = core.reshape(1).astype(jnp.int32)

    def part(x, which, width):
        return lax.dynamic_slice(x, (0, which * width), (x.shape[0], width))

    seg_row = jnp.pad((segment + 1).astype(bf16)[None, :], ((0, SEG_ROWS - 1), (0, half - tok)))
    k_in = swap(jnp.concatenate([part(keys, 1 - core, half), seg_row], 0))
    v_in = swap(part(values, 1 - core, half))
    qg_in = swap(jnp.concatenate([part(queries, 1 - core, q_half), part(grad_out, 1 - core, q_half)], 0))
    seg_both = jnp.concatenate([(segment + 1).astype(bf16), k_in[tok, :tok]])
    both_row = jnp.pad(seg_both[None, :], ((0, SEG_ROWS - 1), (0, half - 2 * tok)))
    kc = jnp.concatenate([part(keys, core, half), k_in[:tok], both_row], 0)
    vc = jnp.concatenate([part(values, core, half), v_in], 0)
    ka = hop(kc, 1)
    va = hop(vc, 1)
    kb = hop(ka, 1)
    vb = hop(va, 1)

    seg_f = seg_both.astype(f32)
    seg0 = jnp.min(seg_f)
    before = jnp.sum((seg_f[:, None] < seg_f[None, :]).astype(jnp.int32), axis=0)
    starts = jnp.where(seg_f == seg0, -1, WINDOW + before).reshape(2, tok)
    lo = jnp.concatenate([starts, jnp.full((6, tok), seg0.astype(jnp.int32), jnp.int32)], 0)

    def at_own(g, c):
        return (0, c[0] * groups + g)

    def at_g(g, c):
        return (0, g)

    def at_seg(g, c):
        return (2 * tok // SEG_ROWS, 0)

    q_block = (tok, 2 * HEAD_DIM)
    kv_block = (2 * tok, HEAD_DIM)
    common_in = [
        pl.BlockSpec((8, tok), lambda g, c: (0, 0)),
        pl.BlockSpec((SEG_ROWS, half), at_seg),
        pl.BlockSpec((SEG_ROWS, half), at_seg),
        pl.BlockSpec(q_block, at_own),
        pl.BlockSpec(q_block, at_g),
        pl.BlockSpec(q_block, at_own),
        pl.BlockSpec(q_block, lambda g, c: (1, g)),
        pl.BlockSpec(kv_block, at_g),
        pl.BlockSpec(kv_block, at_g),
        pl.BlockSpec(kv_block, at_g),
    ]
    common = (core_arr, lo, ka, kb, queries, qg_in, grad_out, qg_in, kb, ka, kc)
    kv_out = [pl.BlockSpec(kv_block, at_g)] * 3
    inv_spec = pl.BlockSpec((1, 8, 2 * tok), lambda g, c: (g, 0, 0))
    kv_shapes = [
        jax.ShapeDtypeStruct((2 * tok, half), bf16),
        jax.ShapeDtypeStruct((2 * tok, half), f32),
        jax.ShapeDtypeStruct((2 * tok, half), f32),
    ]
    blocks = WINDOW // tok + 1
    window = WINDOW + 2 * tok
    tile = pltpu.VMEM((blocks, tok, 2 * tok), f32)
    lo_s = pltpu.VMEM((2, 8, 2 * tok), jnp.int32)
    k_s = pltpu.VMEM((window, HEAD_DIM), bf16)
    acc_s = pltpu.VMEM((window, HEAD_DIM), f32)
    params = pltpu.CompilerParams(vmem_limit_bytes=32 * 1024 * 1024)
    dvb, dva, dvc, inv = pl.pallas_call(
        functools.partial(value_kernel, tok),
        grid_spec=pltpu.PrefetchScalarGridSpec(
            num_scalar_prefetch=1,
            grid=(groups,),
            in_specs=common_in,
            out_specs=kv_out + [inv_spec],
            scratch_shapes=[lo_s, k_s, tile, acc_s],
        ),
        out_shape=kv_shapes + [jax.ShapeDtypeStruct((groups, 8, 2 * tok), f32)],
        compiler_params=params,
        name="value_grads",
    )(*common)
    cv = hop(dvb, -1)
    dkb, dka, dkc, dq0, dq1 = pl.pallas_call(
        functools.partial(score_kernel, tok),
        grid_spec=pltpu.PrefetchScalarGridSpec(
            num_scalar_prefetch=1,
            grid=(groups,),
            in_specs=common_in + [pl.BlockSpec(kv_block, at_g)] * 3 + [inv_spec],
            out_specs=kv_out + [pl.BlockSpec(q_block, at_g)] * 2,
            scratch_shapes=[lo_s, k_s, k_s, tile, tile, tile, acc_s],
        ),
        out_shape=kv_shapes + [jax.ShapeDtypeStruct((tok, q_half), bf16)] * 2,
        compiler_params=params,
        name="score_grads",
    )(*common, vb, va, vc, inv)
    ck = hop(dkb, -1)
    dv = hop((dva + cv.astype(f32)).astype(bf16), -1)
    dk = hop((dka + ck.astype(f32)).astype(bf16), -1)
    sum_v = dvc + dv.astype(f32)
    sum_k = dkc + dk.astype(f32)

    def settle(total):
        mine = total[:tok]
        other = swap(total[tok:].astype(bf16))
        return mine.astype(bf16), other

    def place(mine, other):
        first = jnp.where(core == 0, mine, other)
        second = jnp.where(core == 0, other, mine)
        return jnp.concatenate([first, second], 1)

    grad_q = place(dq0, swap(dq1))
    grad_k = place(*settle(sum_k))
    grad_v = place(*settle(sum_v))
    return grad_q, grad_k, grad_v


def solution(mesh):
    rows = P(AXES, None)
    return jax.shard_map(
        local,
        mesh=mesh,
        in_specs=(rows, rows, rows, rows, P(AXES)),
        out_specs=(rows, rows, rows),
        check_vma=False,
    )
```

```python
import functools

import jax
import jax.numpy as jnp
from jax import lax
from jax.experimental import pallas as pl
from jax.experimental.pallas import tpu as pltpu
from jax.sharding import PartitionSpec as P

HEAD_DIM = 128
WINDOW = 512
SOFTCAP = 50.0
SCALE = 1.0 / 12.0
LOG2E = 1.4426950408889634
AXES = ("ctx", "fsdp")
NT = (((1,), (1,)), ((), ()))
NN = (((1,), (0,)), ((), ()))
SEG_ROWS = 16
FAR = 2


def dot(a, b, dims):
    return lax.dot_general(a, b, dims, preferred_element_type=jnp.float32)


def swap(x):
    n = lax.axis_size(AXES)
    return lax.ppermute(x, AXES, [(i, i ^ 1) for i in range(n)])


def hop(x, chips):
    n = lax.axis_size(AXES)
    by = 2 * chips
    return lax.ppermute(x, AXES, [(i, i + by) for i in range(n) if 0 <= i + by < n])


def rows_at(core, half, tok):
    return pl.ds(pl.multiple_of(lax.bitwise_xor(core, half) * tok, tok), tok)


def lanes_at(g):
    return pl.ds(pl.multiple_of(g * HEAD_DIM, HEAD_DIM), HEAD_DIM)


def block_of(core, pieces, b, g, tok):
    return pieces[b // 2][rows_at(core, b % 2, tok), lanes_at(g)]


def seen(lo, seg_ref, tok):
    ids = seg_ref[2 * tok : 2 * tok + 1, : 2 * tok].astype(jnp.float32)
    same = jnp.where(ids == lo[2:3, 0:1].astype(jnp.float32), 1.0, 0.0)
    return jnp.sum(same, axis=1, keepdims=True).astype(jnp.int32)


def first_keys(core, lo, count, half, tok):
    mine = jnp.where(core == half, lo[0:1], lo[1:2])
    mine = jnp.where(mine < 0, WINDOW - count, mine) - half * tok
    row = lax.broadcasted_iota(jnp.int32, (1, tok), 1)
    mine = jnp.maximum(mine, row + 1)
    return jnp.concatenate([mine, mine], 1)


def weights_of(key_rows, q_rows, lo, jj, last, tok):
    s = dot(key_rows, q_rows, NT)
    t = jnp.tanh(s * (SCALE / SOFTCAP))
    w = jnp.exp2(t * (SOFTCAP * LOG2E))
    pos = lax.broadcasted_iota(jnp.int32, s.shape, 0)
    ok = pos >= lo - jj * tok
    if last:
        col = lax.broadcasted_iota(jnp.int32, s.shape, 1)
        ok = ok & (pos <= jnp.where(col >= tok, col - tok, col))
    w = jnp.where(ok, w, 0.0)
    return w, w * (SCALE - t * t * SCALE)


def fold(x):
    return jnp.sum(x.reshape(x.shape[0] // 8, 8, x.shape[1]), axis=0)


def near_weights(tok, groups, core_ref, lo_ref, q, qx, ka, kc, qs, w_near, u_near, tot):
    core = core_ref[0]
    lo_all = lo_ref[...]
    count = seen(lo_all, ka, tok)
    los = [first_keys(core, lo_all, count, h, tok) for h in range(2)]
    blocks = WINDOW // tok + 1

    def step(g, _):
        for hd in range(2):
            at = (core * groups + g) * 2 + hd
            qs[g, core, pl.ds(hd * tok, tok), :] = q[:, lanes_at(at)]
            qs[g, 1 - core, pl.ds(hd * tok, tok), :] = qx[:tok, lanes_at(g * 2 + hd)]
        for h in range(2):
            q_rows = qs[g, h]
            total = jnp.zeros((8, 2 * tok), jnp.float32)
            for jj in range(FAR, blocks):
                k_blk = block_of(core, (None, ka, kc), h + jj, g, tok)
                w, u = weights_of(k_blk, q_rows, los[h], jj, jj == blocks - 1, tok)
                w_near[g, h, jj - FAR] = w
                u_near[g, h, jj - FAR] = u
                total = total + fold(w)
            tot[g, pl.ds(8 * h, 8), :] = total
        return 0

    lax.fori_loop(0, groups, step, 0)


def near_products(tok, groups, core_ref, go, gox, va, vc, w_near, gs, dp_near, term):
    core = core_ref[0]
    blocks = WINDOW // tok + 1

    def step(g, _):
        for hd in range(2):
            at = (core * groups + g) * 2 + hd
            gs[g, core, pl.ds(hd * tok, tok), :] = go[:, lanes_at(at)]
            gs[g, 1 - core, pl.ds(hd * tok, tok), :] = gox[tok:, lanes_at(g * 2 + hd)]
        for h in range(2):
            g_rows = gs[g, h]
            total = jnp.zeros((8, 2 * tok), jnp.float32)
            for jj in range(FAR, blocks):
                v_blk = block_of(core, (None, va, vc), h + jj, g, tok)
                dp = dot(v_blk, g_rows, NT)
                dp_near[g, h, jj - FAR] = dp
                total = total + fold(w_near[g, h, jj - FAR] * dp)
            term[g, pl.ds(8 * h, 8), :] = total
        return 0

    lax.fori_loop(0, groups, step, 0)


def far_values(tok, groups, core_ref, lo_ref, qs, gs, ka, kb, tot, dvb, w_far, u_far, inv):
    core = core_ref[0]
    lo_all = lo_ref[...]
    count = seen(lo_all, ka, tok) + seen(lo_all, kb, tok)
    los = [first_keys(core, lo_all, count, h, tok) for h in range(2)]

    def step(g, _):
        low = {}
        for h in range(2):
            q_rows = qs[g, h]
            total = tot[g, pl.ds(8 * h, 8), :]
            ws = []
            for jj in range(FAR):
                k_blk = block_of(core, (kb, ka), h + jj, g, tok)
                w, u = weights_of(k_blk, q_rows, los[h], jj, False, tok)
                w_far[g, h, jj] = w
                u_far[g, h, jj] = u
                total = total + fold(w)
                ws.append(w)
            one = 1.0 / jnp.sum(total, axis=0, keepdims=True)
            inv[g, pl.ds(8 * h, 8), :] = jnp.broadcast_to(one, (8, 2 * tok))
            for jj in range(FAR):
                if h + jj < FAR:
                    low[h, jj] = (ws[jj] * one).astype(jnp.bfloat16)
        for b in range(FAR):
            acc = None
            for h in range(2):
                if (h, b - h) in low:
                    part = dot(low[h, b - h], gs[g, h], NN)
                    acc = part if acc is None else acc + part
            dvb[rows_at(core, b % 2, tok), lanes_at(g)] = acc.astype(dvb.dtype)
        return 0

    lax.fori_loop(0, groups, step, 0)


def far_keys(tok, groups, core_ref, qs, gs, va, vb, w_far, u_far, inv, term, dkb, ds_far, row):
    core = core_ref[0]

    def step(g, _):
        for h in range(2):
            g_rows = gs[g, h]
            one = inv[g, pl.ds(8 * h, 1), :]
            total = term[g, pl.ds(8 * h, 8), :]
            dps = []
            for jj in range(FAR):
                v_blk = block_of(core, (vb, va), h + jj, g, tok)
                dp = dot(v_blk, g_rows, NT)
                total = total + fold(w_far[g, h, jj] * dp)
                dps.append(dp)
            mean = one * jnp.sum(total, axis=0, keepdims=True)
            row[g, pl.ds(8 * h, 8), :] = jnp.broadcast_to(mean, (8, 2 * tok))
            for jj in range(FAR):
                ds = (u_far[g, h, jj] * one) * (dps[jj] - mean)
                ds_far[g, h, jj] = ds.astype(jnp.bfloat16)
        for b in range(FAR):
            acc = None
            for h in range(2):
                if 0 <= b - h < FAR:
                    part = dot(ds_far[g, h, b - h], qs[g, h], NN)
                    acc = part if acc is None else acc + part
            dkb[rows_at(core, b % 2, tok), lanes_at(g)] = acc.astype(dkb.dtype)
        return 0

    lax.fori_loop(0, groups, step, 0)


def near_values(tok, groups, core_ref, gs, w_near, w_far, inv, dva, dvc):
    core = core_ref[0]
    blocks = WINDOW // tok + 1

    def step(g, _):
        for b in range(FAR, blocks + 1):
            acc = None
            for h in range(2):
                jj = b - h
                if jj >= blocks:
                    continue
                w = w_far[g, h, jj] if jj < FAR else w_near[g, h, jj - FAR]
                low = (w * inv[g, pl.ds(8 * h, 1), :]).astype(jnp.bfloat16)
                part = dot(low, gs[g, h], NN)
                acc = part if acc is None else acc + part
            out = (None, dva, dvc)[b // 2]
            out[rows_at(core, b % 2, tok), lanes_at(g)] = acc
        return 0

    lax.fori_loop(0, groups, step, 0)


def near_keys(tok, groups, core_ref, qs, kb, ka, kc, u_near, dp_near, ds_far, inv, row,
              dka, dkc, dq0, dq1, ds_s, dq_s):
    core = core_ref[0]
    blocks = WINDOW // tok + 1

    def step(g, _):
        for h in range(2):
            one = inv[g, pl.ds(8 * h, 1), :]
            mean = row[g, pl.ds(8 * h, 1), :]
            dq_t = jnp.zeros((HEAD_DIM, 2 * tok), jnp.float32)
            for jj in range(blocks):
                if jj < FAR:
                    ds = ds_far[g, h, jj]
                else:
                    ds = (u_near[g, h, jj - FAR] * one) * (dp_near[g, h, jj - FAR] - mean)
                    ds = ds.astype(jnp.bfloat16)
                    ds_s[h, jj - FAR] = ds
                k_blk = block_of(core, (kb, ka, kc), h + jj, g, tok)
                dq_t = dq_t + dot(k_blk.T, ds, NN)
            dq_s[lax.bitwise_xor(core, h)] = dq_t.T.astype(jnp.bfloat16)
        for r, dq in enumerate((dq0, dq1)):
            for hd in range(2):
                dq[:, lanes_at(2 * g + hd)] = dq_s[r, hd * tok : (hd + 1) * tok, :]
        for b in range(FAR, blocks + 1):
            acc = None
            for h in range(2):
                jj = b - h
                if jj >= blocks:
                    continue
                ds = ds_far[g, h, jj] if jj < FAR else ds_s[h, jj - FAR]
                part = dot(ds, qs[g, h], NN)
                acc = part if acc is None else acc + part
            out = (None, dka, dkc)[b // 2]
            out[rows_at(core, b % 2, tok), lanes_at(g)] = acc
        return 0

    lax.fori_loop(0, groups, step, 0)


def call(body, tok, groups, args, outs, scratch=()):
    vmem = pl.BlockSpec(memory_space=pltpu.VMEM)
    return pl.pallas_call(
        functools.partial(body, tok, groups),
        in_specs=[pl.BlockSpec(memory_space=pltpu.SMEM)] + [vmem] * (len(args) - 1),
        out_specs=[vmem] * len(outs),
        out_shape=[jax.ShapeDtypeStruct(s, d) for s, d in outs],
        scratch_shapes=list(scratch),
        compiler_params=pltpu.CompilerParams(vmem_limit_bytes=VMEM_LIMIT),
        name=body.__name__,
    )(*args)


VMEM_LIMIT = 24 * 1024 * 1024


def local(queries, keys, values, grad_out, segment):
    tok = queries.shape[0]
    kv_width = keys.shape[1]
    half = kv_width // 2
    groups = half // HEAD_DIM
    q_half = queries.shape[1] // 2
    bf16, f32 = jnp.bfloat16, jnp.float32
    core = lax.rem(lax.axis_index(AXES), 2)
    core_arr = core.reshape(1).astype(jnp.int32)

    def part(x, which, width):
        return lax.dynamic_slice(x, (0, which * width), (x.shape[0], width))

    seg_row = jnp.pad((segment + 1).astype(bf16)[None, :], ((0, SEG_ROWS - 1), (0, half - tok)))
    k_in = swap(jnp.concatenate([part(keys, 1 - core, half), seg_row], 0))
    v_in = swap(part(values, 1 - core, half))
    qg_in = swap(jnp.concatenate([part(queries, 1 - core, q_half), part(grad_out, 1 - core, q_half)], 0))
    seg_both = jnp.concatenate([(segment + 1).astype(bf16), k_in[tok, :tok]])
    both_row = jnp.pad(seg_both[None, :], ((0, SEG_ROWS - 1), (0, half - 2 * tok)))
    kc = jnp.concatenate([part(keys, core, half), k_in[:tok], both_row], 0)
    vc = jnp.concatenate([part(values, core, half), v_in], 0)
    ka = hop(kc, 1)
    va = hop(vc, 1)
    kb = hop(ka, 1)
    vb = hop(va, 1)

    seg_f = seg_both.astype(f32)
    seg0 = jnp.min(seg_f)
    before = jnp.sum((seg_f[:, None] < seg_f[None, :]).astype(jnp.int32), axis=0)
    starts = jnp.where(seg_f == seg0, -1, WINDOW + before).reshape(2, tok)
    lo = jnp.concatenate([starts, jnp.full((6, tok), seg0.astype(jnp.int32), jnp.int32)], 0)

    blocks = WINDOW // tok + 1
    near = (groups, 2, blocks - FAR, tok, 2 * tok)
    far = (groups, 2, FAR, tok, 2 * tok)
    rows = ((groups, 2, 2 * tok, HEAD_DIM), bf16)
    stat = ((groups, 16, 2 * tok), f32)
    kv_f = ((2 * tok, half), f32)
    kv_b = ((2 * tok, half), bf16)
    dq_o = ((tok, q_half), bf16)

    qs, w_near, u_near, tot = call(
        near_weights, tok, groups, (core_arr, lo, queries, qg_in, ka, kc),
        [rows, (near, f32), (near, f32), stat])
    gs, dp_near, term = call(
        near_products, tok, groups, (core_arr, grad_out, qg_in, va, vc, w_near),
        [rows, (near, f32), stat])
    dvb, w_far, u_far, inv = call(
        far_values, tok, groups, (core_arr, lo, qs, gs, ka, kb, tot),
        [kv_b, (far, f32), (far, f32), stat])
    cv = hop(dvb, -1)
    dkb, ds_far, row = call(
        far_keys, tok, groups, (core_arr, qs, gs, va, vb, w_far, u_far, inv, term),
        [kv_b, (far, bf16), stat])
    ck = hop(dkb, -1)
    dva, dvc = call(
        near_values, tok, groups, (core_arr, gs, w_near, w_far, inv), [kv_f, kv_f])
    dv = hop((dva + cv.astype(f32)).astype(bf16), -1)
    dka, dkc, dq0, dq1 = call(
        near_keys, tok, groups,
        (core_arr, qs, kb, ka, kc, u_near, dp_near, ds_far, inv, row),
        [kv_f, kv_f, dq_o, dq_o],
        [pltpu.VMEM((2, blocks - FAR, tok, 2 * tok), bf16), pltpu.VMEM((2, 2 * tok, HEAD_DIM), bf16)])
    dk = hop((dka + ck.astype(f32)).astype(bf16), -1)
    sum_v = dvc + dv.astype(f32)
    sum_k = dkc + dk.astype(f32)

    def settle(total):
        mine = total[:tok]
        other = swap(total[tok:].astype(bf16))
        return mine.astype(bf16), other

    def place(mine, other):
        first = jnp.where(core == 0, mine, other)
        second = jnp.where(core == 0, other, mine)
        return jnp.concatenate([first, second], 1)

    grad_q = place(dq0, swap(dq1))
    grad_k = place(*settle(sum_k))
    grad_v = place(*settle(sum_v))
    return grad_q, grad_k, grad_v


def solution(mesh):
    rows = P(AXES, None)
    return jax.shard_map(
        local,
        mesh=mesh,
        in_specs=(rows, rows, rows, rows, P(AXES)),
        out_specs=(rows, rows, rows),
        check_vma=False,
    )
```

```python
import functools

import jax
import jax.numpy as jnp
from jax import lax
from jax.experimental import pallas as pl
from jax.experimental.pallas import tpu as pltpu
from jax.sharding import PartitionSpec as P

HEAD_DIM = 128
WINDOW = 512
SOFTCAP = 50.0
SCALE = 1.0 / 12.0
LOG2E = 1.4426950408889634
AXES = ("ctx", "fsdp")
NT = (((1,), (1,)), ((), ()))
NN = (((1,), (0,)), ((), ()))
SEG_ROWS = 16
FAR = 2


def dot(a, b, dims):
    return lax.dot_general(a, b, dims, preferred_element_type=jnp.float32)


def swap(x):
    n = lax.axis_size(AXES)
    return lax.ppermute(x, AXES, [(i, i ^ 1) for i in range(n)])


def hop(x, chips):
    n = lax.axis_size(AXES)
    by = 2 * chips
    return lax.ppermute(x, AXES, [(i, i + by) for i in range(n) if 0 <= i + by < n])


def cross(x, chips):
    n = lax.axis_size(AXES)
    by = 2 * chips
    return lax.ppermute(x, AXES, [(i, (i ^ 1) + by) for i in range(n) if 0 <= i + by < n])


def rows_at(core, half, tok):
    return pl.ds(pl.multiple_of(lax.bitwise_xor(core, half) * tok, tok), tok)


def lanes_at(g):
    return pl.ds(pl.multiple_of(g * HEAD_DIM, HEAD_DIM), HEAD_DIM)


def block_of(core, pieces, b, g, tok):
    return pieces[b // 2][rows_at(core, b % 2, tok), lanes_at(g)]


def seen(lo, seg_ref, tok):
    ids = seg_ref[2 * tok : 2 * tok + 1, : 2 * tok].astype(jnp.float32)
    same = jnp.where(ids == lo[2:3, 0:1].astype(jnp.float32), 1.0, 0.0)
    return jnp.sum(same, axis=1, keepdims=True).astype(jnp.int32)


def first_keys(core, lo, count, half, tok):
    mine = jnp.where(core == half, lo[0:1], lo[1:2])
    mine = jnp.where(mine < 0, WINDOW - count, mine) - half * tok
    row = lax.broadcasted_iota(jnp.int32, (1, tok), 1)
    mine = jnp.maximum(mine, row + 1)
    return jnp.concatenate([mine, mine], 1)


def keys_of(core, pieces, blocks, g, tok):
    return jnp.concatenate([block_of(core, pieces, b, g, tok) for b in blocks], 0)


def weights_of(s, lo, jj, last, tok):
    t = jnp.tanh(s * (SCALE / SOFTCAP))
    w = jnp.exp2(t * (SOFTCAP * LOG2E))
    pos = lax.broadcasted_iota(jnp.int32, s.shape, 0)
    ok = pos >= lo - jj * tok
    if last:
        col = lax.broadcasted_iota(jnp.int32, s.shape, 1)
        ok = ok & (pos <= jnp.where(col >= tok, col - tok, col))
    return t, jnp.where(ok, w, 0.0)


def slope(t):
    return SCALE - t * t * SCALE


def cut(x, i, tok):
    return x[i * tok : (i + 1) * tok]


def fold(x):
    return jnp.sum(x.reshape(x.shape[0] // 8, 8, x.shape[1]), axis=0)


def stack_heads(tok, groups, core_ref, q, go, qgx, qs, gs):
    core = core_ref[0]
    for g in range(groups):
        for hd in range(2):
            at = (core * groups + g) * 2 + hd
            here = pl.ds(hd * tok, tok)
            qs[g, core, here, :] = q[:, lanes_at(at)]
            gs[g, core, here, :] = go[:, lanes_at(at)]
            qs[g, 1 - core, here, :] = qgx[:tok, lanes_at(g * 2 + hd)]
            gs[g, 1 - core, here, :] = qgx[tok:, lanes_at(g * 2 + hd)]


def near_sums(tok, groups, core_ref, lo_ref, qs, gs, ka, kc, va, vc, tot, term):
    core = core_ref[0]
    lo_all = lo_ref[...]
    count = seen(lo_all, ka, tok)
    los = [first_keys(core, lo_all, count, h, tok) for h in range(2)]
    blocks = WINDOW // tok + 1

    def step(g, _):
        for h in range(2):
            near = range(h + FAR, h + blocks)
            s = dot(keys_of(core, (None, ka, kc), near, g, tok), qs[g, h], NT)
            dp = dot(keys_of(core, (None, va, vc), near, g, tok), gs[g, h], NT)
            total = jnp.zeros((8, 2 * tok), jnp.float32)
            mean = jnp.zeros((8, 2 * tok), jnp.float32)
            for jj in range(FAR, blocks):
                _, w = weights_of(cut(s, jj - FAR, tok), los[h], jj, jj == blocks - 1, tok)
                total = total + fold(w)
                mean = mean + fold(w * cut(dp, jj - FAR, tok))
            tot[g, pl.ds(8 * h, 8), :] = total
            term[g, pl.ds(8 * h, 8), :] = mean
        return 0

    lax.fori_loop(0, groups, step, 0, unroll=True)


def far_values(tok, groups, core_ref, lo_ref, qs, gs, ka, kb, tot, dvb, inv):
    core = core_ref[0]
    lo_all = lo_ref[...]
    count = seen(lo_all, ka, tok) + seen(lo_all, kb, tok)
    los = [first_keys(core, lo_all, count, h, tok) for h in range(2)]

    def step(g, _):
        accs = []
        for h in range(2):
            s = dot(keys_of(core, (kb, ka), range(h, h + FAR), g, tok), qs[g, h], NT)
            total = tot[g, pl.ds(8 * h, 8), :]
            ws = []
            for jj in range(FAR):
                _, w = weights_of(cut(s, jj, tok), los[h], jj, False, tok)
                total = total + fold(w)
                ws.append(w)
            one = 1.0 / jnp.sum(total, axis=0, keepdims=True)
            inv[g, pl.ds(8 * h, 8), :] = jnp.broadcast_to(one, (8, 2 * tok))
            low = jnp.concatenate([(w * one).astype(jnp.bfloat16) for w in ws[: FAR - h]], 0)
            accs.append(dot(low, gs[g, h], NN))
        spread(core, accs, 0, (dvb,), g, tok)
        return 0

    lax.fori_loop(0, groups, step, 0, unroll=True)


def spread(core, accs, start, outs, g, tok):
    first = (start, max(start, 1))
    for b in range(start, start + 2 * len(outs)):
        acc = None
        for h in range(2):
            i = b - first[h]
            if 0 <= i < accs[h].shape[0] // tok:
                piece = cut(accs[h], i, tok)
                acc = piece if acc is None else acc + piece
        out = outs[(b - start) // 2]
        out[rows_at(core, b % 2, tok), lanes_at(g)] = acc.astype(out.dtype)


def far_keys(tok, groups, core_ref, lo_ref, qs, gs, ka, kb, va, vb, inv, term, dkb, row):
    core = core_ref[0]
    lo_all = lo_ref[...]
    count = seen(lo_all, ka, tok) + seen(lo_all, kb, tok)
    los = [first_keys(core, lo_all, count, h, tok) for h in range(2)]

    def step(g, _):
        accs = []
        for h in range(2):
            s = dot(keys_of(core, (kb, ka), range(h, h + FAR), g, tok), qs[g, h], NT)
            dp = dot(keys_of(core, (vb, va), range(h, h + FAR), g, tok), gs[g, h], NT)
            one = inv[g, pl.ds(8 * h, 1), :]
            total = term[g, pl.ds(8 * h, 8), :]
            us = []
            for jj in range(FAR):
                t, w = weights_of(cut(s, jj, tok), los[h], jj, False, tok)
                total = total + fold(w * cut(dp, jj, tok))
                us.append(w * slope(t))
            mean = one * jnp.sum(total, axis=0, keepdims=True)
            row[g, pl.ds(8 * h, 8), :] = jnp.broadcast_to(mean, (8, 2 * tok))
            low = [((us[jj] * one) * (cut(dp, jj, tok) - mean)).astype(jnp.bfloat16) for jj in range(FAR - h)]
            accs.append(dot(jnp.concatenate(low, 0), qs[g, h], NN))
        spread(core, accs, 0, (dkb,), g, tok)
        return 0

    lax.fori_loop(0, groups, step, 0, unroll=True)


def near_grads(tok, groups, core_ref, lo_ref, qs, gs, kb, ka, kc, vb, va, vc, inv, row,
               dva, dvc, dka, dkc, dq0, dq1, dq_s):
    core = core_ref[0]
    lo_all = lo_ref[...]
    count = seen(lo_all, ka, tok) + seen(lo_all, kb, tok)
    los = [first_keys(core, lo_all, count, h, tok) for h in range(2)]
    blocks = WINDOW // tok + 1

    def step(g, _):
        dvs, dks = [], []
        for h in range(2):
            k_rows = keys_of(core, (kb, ka, kc), range(h, h + blocks), g, tok)
            v_rows = keys_of(core, (vb, va, vc), range(h, h + blocks), g, tok)
            s = dot(k_rows, qs[g, h], NT)
            dp = dot(v_rows, gs[g, h], NT)
            one = inv[g, pl.ds(8 * h, 1), :]
            mean = row[g, pl.ds(8 * h, 1), :]
            low, dlow = [], []
            for jj in range(blocks):
                t, w = weights_of(cut(s, jj, tok), los[h], jj, jj == blocks - 1, tok)
                p = w * one
                low.append(p.astype(jnp.bfloat16))
                ds = p * slope(t) * (cut(dp, jj, tok) - mean)
                dlow.append(ds.astype(jnp.bfloat16))
            dvs.append(dot(jnp.concatenate(low[FAR - h :], 0), gs[g, h], NN))
            dks.append(dot(jnp.concatenate(dlow[FAR - h :], 0), qs[g, h], NN))
            dq_t = dot(k_rows.T, jnp.concatenate(dlow, 0), NN)
            dq_s[g, lax.bitwise_xor(core, h)] = dq_t.T.astype(jnp.bfloat16)
        spread(core, dvs, FAR, (dva, dvc), g, tok)
        spread(core, dks, FAR, (dka, dkc), g, tok)
        for r, dq in enumerate((dq0, dq1)):
            for hd in range(2):
                dq[:, lanes_at(2 * g + hd)] = dq_s[g, r, hd * tok : (hd + 1) * tok, :]
        return 0

    lax.fori_loop(0, groups, step, 0, unroll=True)


def call(body, tok, groups, args, outs, scratch=()):
    vmem = pl.BlockSpec(memory_space=pltpu.VMEM)
    return pl.pallas_call(
        functools.partial(body, tok, groups),
        in_specs=[pl.BlockSpec(memory_space=pltpu.SMEM)] + [vmem] * (len(args) - 1),
        out_specs=[vmem] * len(outs),
        out_shape=[jax.ShapeDtypeStruct(s, d) for s, d in outs],
        scratch_shapes=list(scratch),
        compiler_params=pltpu.CompilerParams(vmem_limit_bytes=VMEM_LIMIT),
        name=body.__name__,
    )(*args)


VMEM_LIMIT = 4 * 1024 * 1024


def local(queries, keys, values, grad_out, segment):
    tok = queries.shape[0]
    kv_width = keys.shape[1]
    half = kv_width // 2
    groups = half // HEAD_DIM
    q_half = queries.shape[1] // 2
    bf16, f32 = jnp.bfloat16, jnp.float32
    core = lax.rem(lax.axis_index(AXES), 2)
    core_arr = core.reshape(1).astype(jnp.int32)

    def part(x, which, width):
        return lax.dynamic_slice(x, (0, which * width), (x.shape[0], width))

    seg_own = (segment + 1).astype(bf16)[None, :]
    seg_row = jnp.pad(seg_own, ((0, SEG_ROWS - 1), (0, half - tok)))
    own_row = jnp.pad(seg_own, ((0, SEG_ROWS - 1), (tok, half - 2 * tok)))
    k_out = jnp.concatenate([part(keys, 1 - core, half), seg_row], 0)
    k_in = swap(k_out)
    kc = jnp.concatenate([part(keys, core, half), k_in[:tok], k_in[tok:] + own_row], 0)
    values, _ = lax.optimization_barrier((values, kc))
    v_in = swap(part(values, 1 - core, half))
    vc = jnp.concatenate([part(values, core, half), v_in], 0)
    ka = hop(kc, 1)
    va = hop(vc, 1)
    queries, grad_out, _ = lax.optimization_barrier((queries, grad_out, kc))
    qg_in = swap(jnp.concatenate([part(queries, 1 - core, q_half), part(grad_out, 1 - core, q_half)], 0))

    seg_f = jnp.concatenate([seg_own[0], k_in[tok, :tok]]).astype(f32)
    seg0 = jnp.min(seg_f)
    before = jnp.sum((seg_f[:, None] < seg_f[None, :]).astype(jnp.int32), axis=0)
    starts = jnp.where(seg_f == seg0, -1, WINDOW + before).reshape(2, tok)
    lo = jnp.concatenate([starts, jnp.full((6, tok), seg0.astype(jnp.int32), jnp.int32)], 0)

    rows = ((groups, 2, 2 * tok, HEAD_DIM), bf16)
    stat = ((groups, 16, 2 * tok), f32)
    kv_f = ((2 * tok, half), f32)
    kv_b = ((2 * tok, half), bf16)
    dq_o = ((tok, q_half), bf16)

    qs, gs = call(stack_heads, tok, groups, (core_arr, queries, grad_out, qg_in), [rows, rows])
    va, qs, gs, lo = lax.optimization_barrier((va, qs, gs, lo))
    kb = hop(ka, 1)
    vb = hop(va, 1)
    tot, term = call(
        near_sums, tok, groups, (core_arr, lo, qs, gs, ka, kc, va, vc), [stat, stat])
    dvb, inv = call(
        far_values, tok, groups, (core_arr, lo, qs, gs, ka, kb, tot), [kv_b, stat])
    cv = hop(dvb, -1)
    dkb, row = call(
        far_keys, tok, groups, (core_arr, lo, qs, gs, ka, kb, va, vb, inv, term), [kv_b, stat])
    ck = hop(dkb, -1)
    dva, dvc, dka, dkc, dq0, dq1 = call(
        near_grads, tok, groups, (core_arr, lo, qs, gs, kb, ka, kc, vb, va, vc, inv, row),
        [kv_f, kv_f, kv_f, kv_f, dq_o, dq_o],
        [pltpu.VMEM((groups, 2, 2 * tok, HEAD_DIM), bf16)])
    dv = hop((dva + cv.astype(f32)).astype(bf16), -1)
    dk_out = (dka + ck.astype(f32)).astype(bf16)
    dk_same = hop(dk_out[:tok], -1)
    dk_cross = cross(dk_out[tok:], -1)
    def place(mine, other):
        first = jnp.where(core == 0, mine, other)
        second = jnp.where(core == 0, other, mine)
        return jnp.concatenate([first, second], 1)

    grad_q = place(dq0, swap(dq1))
    sum_v = dvc + dv.astype(f32)
    grad_v = place(sum_v[:tok].astype(bf16), swap(sum_v[tok:].astype(bf16)))
    other_k = swap(dkc[tok:])
    same = (dkc[:tok] + dk_same.astype(f32)).astype(bf16)
    other = (other_k + dk_cross.astype(f32)).astype(bf16)
    grad_k = place(same, other)
    return grad_q, grad_k, grad_v


def solution(mesh):
    rows = P(AXES, None)
    return jax.shard_map(
        local,
        mesh=mesh,
        in_specs=(rows, rows, rows, rows, P(AXES)),
        out_specs=(rows, rows, rows),
        check_vma=False,
    )
```

```python
import functools

import jax
import jax.numpy as jnp
from jax import lax
from jax.experimental import pallas as pl
from jax.experimental.pallas import tpu as pltpu
from jax.sharding import PartitionSpec as P

HEAD_DIM = 128
WINDOW = 512
SOFTCAP = 50.0
SCALE = 1.0 / 12.0
LOG2E = 1.4426950408889634
AXES = ("ctx", "fsdp")
NT = (((1,), (1,)), ((), ()))
NN = (((1,), (0,)), ((), ()))
SEG_ROWS = 16
FAR = 2


def dot(a, b, dims):
    return lax.dot_general(a, b, dims, preferred_element_type=jnp.float32)


def swap(x):
    n = lax.axis_size(AXES)
    return lax.ppermute(x, AXES, [(i, i ^ 1) for i in range(n)])


def hop(x, chips):
    n = lax.axis_size(AXES)
    by = 2 * chips
    return lax.ppermute(x, AXES, [(i, i + by) for i in range(n) if 0 <= i + by < n])


def cross(x, chips):
    n = lax.axis_size(AXES)
    by = 2 * chips
    return lax.ppermute(x, AXES, [(i, (i ^ 1) + by) for i in range(n) if 0 <= i + by < n])


def forward(x):
    n, row = lax.axis_size(AXES), lax.axis_size("fsdp")
    return lax.ppermute(x, AXES, [(i, i + 2) for i in range(n) if i % row < row - 2])


def ahead(x):
    n, row = lax.axis_size(AXES), lax.axis_size("fsdp")
    return lax.ppermute(x, AXES, [(i, i + 4) for i in range(n - 4) if row - 4 <= i % row < row - 2])


def rows_at(core, half, tok):
    return pl.ds(pl.multiple_of(lax.bitwise_xor(core, half) * tok, tok), tok)


def lanes_at(g):
    return pl.ds(pl.multiple_of(g * HEAD_DIM, HEAD_DIM), HEAD_DIM)


def block_of(core, pieces, b, g, tok):
    parts = pieces[b // 2]
    at = (rows_at(core, b % 2, tok), lanes_at(g))
    return parts[0][at] + parts[1][at] if isinstance(parts, tuple) else parts[at]


def seen(lo, seg_ref, tok):
    ids = seg_ref[2 * tok : 2 * tok + 1, : 2 * tok].astype(jnp.float32)
    same = jnp.where(ids == lo[2:3, 0:1].astype(jnp.float32), 1.0, 0.0)
    return jnp.sum(same, axis=1, keepdims=True).astype(jnp.int32)


def first_keys(core, lo, count, half, tok):
    mine = jnp.where(core == half, lo[0:1], lo[1:2])
    mine = jnp.where(mine < 0, WINDOW - count, mine) - half * tok
    row = lax.broadcasted_iota(jnp.int32, (1, tok), 1)
    mine = jnp.maximum(mine, row + 1)
    return jnp.concatenate([mine, mine], 1)


def keys_of(core, pieces, blocks, g, tok):
    return jnp.concatenate([block_of(core, pieces, b, g, tok) for b in blocks], 0)


def weights_of(s, lo, jj, last, tok):
    t = jnp.tanh(s * (SCALE / SOFTCAP))
    w = jnp.exp2(t * (SOFTCAP * LOG2E))
    pos = lax.broadcasted_iota(jnp.int32, s.shape, 0)
    ok = pos >= lo - jj * tok
    if last:
        col = lax.broadcasted_iota(jnp.int32, s.shape, 1)
        ok = ok & (pos <= jnp.where(col >= tok, col - tok, col))
    return t, jnp.where(ok, w, 0.0)


def slope(t):
    return SCALE - t * t * SCALE


def cut(x, i, tok):
    return x[i * tok : (i + 1) * tok]


def fold(x):
    return jnp.sum(x.reshape(x.shape[0] // 8, 8, x.shape[1]), axis=0)


def stack_heads(tok, groups, core_ref, q, go, qgx, kc, qs, gs, lo):
    core = core_ref[0]
    ids = kc[2 * tok : 2 * tok + 1, : 2 * tok].astype(jnp.float32)
    column = jnp.broadcast_to(ids, (8, 2 * tok)).T[:, 0:1]
    before = jnp.sum(jnp.where(column < ids, 1.0, 0.0), axis=0, keepdims=True)
    first = jnp.min(ids, axis=1, keepdims=True)
    starts = jnp.where(ids == first, -1.0, WINDOW + before).astype(jnp.int32)
    lo[0:1, :] = starts[:, :tok]
    lo[1:2, :] = starts[:, tok:]
    lo[2:8, :] = jnp.broadcast_to(first.astype(jnp.int32), (6, tok))
    for g in range(groups):
        for hd in range(2):
            at = (core * groups + g) * 2 + hd
            here = pl.ds(hd * tok, tok)
            qs[g, core, here, :] = q[:, lanes_at(at)]
            gs[g, core, here, :] = go[:, lanes_at(at)]
            qs[g, 1 - core, here, :] = qgx[:tok, lanes_at(g * 2 + hd)]
            gs[g, 1 - core, here, :] = qgx[tok:, lanes_at(g * 2 + hd)]


def near_sums(tok, groups, core_ref, lo_ref, qs, gs, ka, kc, va, vc, tot, term):
    core = core_ref[0]
    lo_all = lo_ref[...]
    count = seen(lo_all, ka, tok)
    los = [first_keys(core, lo_all, count, h, tok) for h in range(2)]
    blocks = WINDOW // tok + 1

    def step(g, _):
        for h in range(2):
            near = range(h + FAR, h + blocks)
            s = dot(keys_of(core, (None, ka, kc), near, g, tok), qs[g, h], NT)
            dp = dot(keys_of(core, (None, va, vc), near, g, tok), gs[g, h], NT)
            total = jnp.zeros((8, 2 * tok), jnp.float32)
            mean = jnp.zeros((8, 2 * tok), jnp.float32)
            for jj in range(FAR, blocks):
                _, w = weights_of(cut(s, jj - FAR, tok), los[h], jj, jj == blocks - 1, tok)
                total = total + fold(w)
                mean = mean + fold(w * cut(dp, jj - FAR, tok))
            tot[g, pl.ds(8 * h, 8), :] = total
            term[g, pl.ds(8 * h, 8), :] = mean
        return 0

    lax.fori_loop(0, groups, step, 0, unroll=True)


def far_values(tok, groups, core_ref, lo_ref, qs, gs, ka, kb, wk, tot, dvb, inv):
    core = core_ref[0]
    lo_all = lo_ref[...]
    count = seen(lo_all, ka, tok) + seen(lo_all, kb, tok) + seen(lo_all, wk, tok)
    los = [first_keys(core, lo_all, count, h, tok) for h in range(2)]

    def step(g, _):
        accs = []
        for h in range(2):
            s = dot(keys_of(core, ((kb, wk), ka), range(h, h + FAR), g, tok), qs[g, h], NT)
            total = tot[g, pl.ds(8 * h, 8), :]
            ws = []
            for jj in range(FAR):
                _, w = weights_of(cut(s, jj, tok), los[h], jj, False, tok)
                total = total + fold(w)
                ws.append(w)
            one = 1.0 / jnp.sum(total, axis=0, keepdims=True)
            inv[g, pl.ds(8 * h, 8), :] = jnp.broadcast_to(one, (8, 2 * tok))
            low = jnp.concatenate([(w * one).astype(jnp.bfloat16) for w in ws[: FAR - h]], 0)
            accs.append(dot(low, gs[g, h], NN))
        spread(core, accs, 0, (dvb,), g, tok)
        return 0

    lax.fori_loop(0, groups, step, 0, unroll=True)


def spread(core, accs, start, outs, g, tok):
    first = (start, max(start, 1))
    for b in range(start, start + 2 * len(outs)):
        acc = None
        for h in range(2):
            i = b - first[h]
            if 0 <= i < accs[h].shape[0] // tok:
                piece = cut(accs[h], i, tok)
                acc = piece if acc is None else acc + piece
        out = outs[(b - start) // 2]
        out[rows_at(core, b % 2, tok), lanes_at(g)] = acc.astype(out.dtype)


def far_keys(tok, groups, core_ref, lo_ref, qs, gs, ka, kb, wk, va, vb, wv, inv, term, dkb, row):
    core = core_ref[0]
    lo_all = lo_ref[...]
    count = seen(lo_all, ka, tok) + seen(lo_all, kb, tok) + seen(lo_all, wk, tok)
    los = [first_keys(core, lo_all, count, h, tok) for h in range(2)]

    def step(g, _):
        accs = []
        for h in range(2):
            s = dot(keys_of(core, ((kb, wk), ka), range(h, h + FAR), g, tok), qs[g, h], NT)
            dp = dot(keys_of(core, ((vb, wv), va), range(h, h + FAR), g, tok), gs[g, h], NT)
            one = inv[g, pl.ds(8 * h, 1), :]
            total = term[g, pl.ds(8 * h, 8), :]
            us = []
            for jj in range(FAR):
                t, w = weights_of(cut(s, jj, tok), los[h], jj, False, tok)
                total = total + fold(w * cut(dp, jj, tok))
                us.append(w * slope(t))
            mean = one * jnp.sum(total, axis=0, keepdims=True)
            row[g, pl.ds(8 * h, 8), :] = jnp.broadcast_to(mean, (8, 2 * tok))
            low = [((us[jj] * one) * (cut(dp, jj, tok) - mean)).astype(jnp.bfloat16) for jj in range(FAR - h)]
            accs.append(dot(jnp.concatenate(low, 0), qs[g, h], NN))
        spread(core, accs, 0, (dkb,), g, tok)
        return 0

    lax.fori_loop(0, groups, step, 0, unroll=True)


def near_grads(tok, groups, core_ref, lo_ref, qs, gs, kb, wk, ka, kc, vb, wv, va, vc, inv, row,
               dva, dvc, dka, dkc, dq0, dq1, dq_s):
    core = core_ref[0]
    lo_all = lo_ref[...]
    count = seen(lo_all, ka, tok) + seen(lo_all, kb, tok) + seen(lo_all, wk, tok)
    los = [first_keys(core, lo_all, count, h, tok) for h in range(2)]
    blocks = WINDOW // tok + 1

    def step(g, _):
        dvs, dks = [], []
        for h in range(2):
            k_rows = keys_of(core, ((kb, wk), ka, kc), range(h, h + blocks), g, tok)
            v_rows = keys_of(core, ((vb, wv), va, vc), range(h, h + blocks), g, tok)
            s = dot(k_rows, qs[g, h], NT)
            dp = dot(v_rows, gs[g, h], NT)
            one = inv[g, pl.ds(8 * h, 1), :]
            mean = row[g, pl.ds(8 * h, 1), :]
            low, dlow = [], []
            for jj in range(blocks):
                t, w = weights_of(cut(s, jj, tok), los[h], jj, jj == blocks - 1, tok)
                p = w * one
                low.append(p.astype(jnp.bfloat16))
                ds = p * slope(t) * (cut(dp, jj, tok) - mean)
                dlow.append(ds.astype(jnp.bfloat16))
            dvs.append(dot(jnp.concatenate(low[FAR - h :], 0), gs[g, h], NN))
            dks.append(dot(jnp.concatenate(dlow[FAR - h :], 0), qs[g, h], NN))
            dq_t = dot(k_rows.T, jnp.concatenate(dlow, 0), NN)
            dq_s[g, lax.bitwise_xor(core, h)] = dq_t.T.astype(jnp.bfloat16)
        spread(core, dvs, FAR, (dva, dvc), g, tok)
        spread(core, dks, FAR, (dka, dkc), g, tok)
        for r, dq in enumerate((dq0, dq1)):
            for hd in range(2):
                dq[:, lanes_at(2 * g + hd)] = dq_s[g, r, hd * tok : (hd + 1) * tok, :]
        return 0

    lax.fori_loop(0, groups, step, 0, unroll=True)


def call(body, tok, groups, args, outs, scratch=()):
    vmem = pl.BlockSpec(memory_space=pltpu.VMEM)
    return pl.pallas_call(
        functools.partial(body, tok, groups),
        in_specs=[pl.BlockSpec(memory_space=pltpu.SMEM)] + [vmem] * (len(args) - 1),
        out_specs=[vmem] * len(outs),
        out_shape=[jax.ShapeDtypeStruct(s, d) for s, d in outs],
        scratch_shapes=list(scratch),
        compiler_params=pltpu.CompilerParams(vmem_limit_bytes=VMEM_LIMIT),
        name=body.__name__,
    )(*args)


VMEM_LIMIT = 4 * 1024 * 1024


def local(queries, keys, values, grad_out, segment):
    tok = queries.shape[0]
    kv_width = keys.shape[1]
    half = kv_width // 2
    groups = half // HEAD_DIM
    q_half = queries.shape[1] // 2
    bf16, f32 = jnp.bfloat16, jnp.float32
    core = lax.rem(lax.axis_index(AXES), 2)
    core_arr = core.reshape(1).astype(jnp.int32)

    def part(x, which, width):
        return lax.dynamic_slice(x, (0, which * width), (x.shape[0], width))

    seg_own = (segment + 1).astype(bf16)[None, :]
    seg_row = jnp.pad(seg_own, ((0, SEG_ROWS - 1), (tok, half - 2 * tok)))
    own_row = jnp.pad(seg_own, ((0, SEG_ROWS - 1), (0, half - tok)))
    k_in = swap(jnp.concatenate([part(keys, 1 - core, half), seg_row], 0))
    kc = jnp.concatenate([part(keys, core, half), k_in[:tok], k_in[tok:] + own_row], 0)
    values, _ = lax.optimization_barrier((values, kc))
    v_in = swap(part(values, 1 - core, half))
    vc = jnp.concatenate([part(values, core, half), v_in, jnp.zeros((16, half), bf16)], 0)
    ka = hop(kc, 1)
    va = hop(vc, 1)
    queries, grad_out, _ = lax.optimization_barrier((queries, grad_out, kc))
    qg_in = swap(jnp.concatenate([part(queries, 1 - core, q_half), part(grad_out, 1 - core, q_half)], 0))

    rows = ((groups, 2, 2 * tok, HEAD_DIM), bf16)
    stat = ((groups, 16, 2 * tok), f32)
    kv_f = ((2 * tok, half), f32)
    kv_b = ((2 * tok, half), bf16)
    dq_o = ((tok, q_half), bf16)

    qs, gs, lo = call(
        stack_heads, tok, groups, (core_arr, queries, grad_out, qg_in, kc),
        [rows, rows, ((8, tok), jnp.int32)])
    va, qs, gs, lo = lax.optimization_barrier((va, qs, gs, lo))
    wk = ahead(kc)
    wv = ahead(vc)
    kb = forward(ka)
    vb = forward(va)
    tot, term = call(
        near_sums, tok, groups, (core_arr, lo, qs, gs, ka, kc, va, vc), [stat, stat])
    dvb, inv = call(
        far_values, tok, groups, (core_arr, lo, qs, gs, ka, kb, wk, tot), [kv_b, stat])
    cv = hop(dvb, -1)
    dkb, row = call(
        far_keys, tok, groups, (core_arr, lo, qs, gs, ka, kb, wk, va, vb, wv, inv, term), [kv_b, stat])
    ck = hop(dkb, -1)
    dva, dvc, dka, dkc, dq0, dq1 = call(
        near_grads, tok, groups, (core_arr, lo, qs, gs, kb, wk, ka, kc, vb, wv, va, vc, inv, row),
        [kv_f, kv_f, kv_f, kv_f, dq_o, dq_o],
        [pltpu.VMEM((groups, 2, 2 * tok, HEAD_DIM), bf16)])
    dv = hop((dva + cv.astype(f32)).astype(bf16), -1)
    dk_out = (dka + ck.astype(f32)).astype(bf16)
    dk_same = hop(dk_out[:tok], -1)
    dk_cross = cross(dk_out[tok:], -1)
    def place(mine, other):
        first = jnp.where(core == 0, mine, other)
        second = jnp.where(core == 0, other, mine)
        return jnp.concatenate([first, second], 1)

    grad_q = place(dq0, swap(dq1))
    sum_v = dvc + dv.astype(f32)
    grad_v = place(sum_v[:tok].astype(bf16), swap(sum_v[tok:].astype(bf16)))
    other_k = swap(dkc[tok:])
    dk_cross, grad_v = lax.optimization_barrier((dk_cross, grad_v))
    same = (dkc[:tok] + dk_same.astype(f32)).astype(bf16)
    other = (other_k + dk_cross.astype(f32)).astype(bf16)
    grad_k = place(same, other)
    return grad_q, grad_k, grad_v


def solution(mesh):
    rows = P(AXES, None)
    return jax.shard_map(
        local,
        mesh=mesh,
        in_specs=(rows, rows, rows, rows, P(AXES)),
        out_specs=(rows, rows, rows),
        check_vma=False,
    )
```

```python
import functools

import jax
import jax.numpy as jnp
from jax import lax
from jax.experimental import pallas as pl
from jax.experimental.pallas import tpu as pltpu
from jax.sharding import PartitionSpec as P

HEAD_DIM = 128
WINDOW = 512
SOFTCAP = 50.0
SCALE = 1.0 / 12.0
LOG2E = 1.4426950408889634
AXES = ("ctx", "fsdp")
NT = (((1,), (1,)), ((), ()))
NN = (((1,), (0,)), ((), ()))
SEG_ROWS = 16
FAR = 2


def dot(a, b, dims):
    return lax.dot_general(a, b, dims, preferred_element_type=jnp.float32)


def swap(x):
    n = lax.axis_size(AXES)
    return lax.ppermute(x, AXES, [(i, i ^ 1) for i in range(n)])


def hop(x, chips):
    n = lax.axis_size(AXES)
    by = 2 * chips
    return lax.ppermute(x, AXES, [(i, i + by) for i in range(n) if 0 <= i + by < n])


def cross(x, chips):
    n = lax.axis_size(AXES)
    by = 2 * chips
    return lax.ppermute(x, AXES, [(i, (i ^ 1) + by) for i in range(n) if 0 <= i + by < n])


def forward(x):
    n, row = lax.axis_size(AXES), lax.axis_size("fsdp")
    return lax.ppermute(x, AXES, [(i, i + 2) for i in range(n) if i % row < row - 2])


def ahead(x):
    n, row = lax.axis_size(AXES), lax.axis_size("fsdp")
    return lax.ppermute(x, AXES, [(i, i + 4) for i in range(n - 4) if row - 4 <= i % row < row - 2])


def rows_at(core, half, tok):
    return pl.ds(pl.multiple_of(lax.bitwise_xor(core, half) * tok, tok), tok)


def lanes_at(g):
    return pl.ds(pl.multiple_of(g * HEAD_DIM, HEAD_DIM), HEAD_DIM)


def block_of(core, pieces, b, g, tok):
    parts = pieces[b // 2]
    at = (rows_at(core, b % 2, tok), lanes_at(g))
    return parts[0][at] + parts[1][at] if isinstance(parts, tuple) else parts[at]


def seen(lo, seg_ref, tok):
    ids = seg_ref[2 * tok : 2 * tok + 1, : 2 * tok].astype(jnp.float32)
    same = jnp.where(ids == lo[2:3, 0:1].astype(jnp.float32), 1.0, 0.0)
    return jnp.sum(same, axis=1, keepdims=True).astype(jnp.int32)


def first_keys(core, lo, count, half, tok):
    mine = jnp.where(core == half, lo[0:1], lo[1:2])
    mine = jnp.where(mine < 0, WINDOW - count, mine) - half * tok
    row = lax.broadcasted_iota(jnp.int32, (1, tok), 1)
    mine = jnp.maximum(mine, row + 1)
    return jnp.concatenate([mine, mine], 1)


def keys_of(core, pieces, blocks, g, tok):
    return jnp.concatenate([block_of(core, pieces, b, g, tok) for b in blocks], 0)


def weights_of(s, lo, jj, last, tok):
    t = jnp.tanh(s * (SCALE / SOFTCAP))
    w = jnp.exp2(t * (SOFTCAP * LOG2E))
    pos = lax.broadcasted_iota(jnp.int32, s.shape, 0)
    ok = pos >= lo - jj * tok
    if last:
        col = lax.broadcasted_iota(jnp.int32, s.shape, 1)
        ok = ok & (pos <= jnp.where(col >= tok, col - tok, col))
    return t, jnp.where(ok, w, 0.0)


def slope(t):
    return SCALE - t * t * SCALE


def cut(x, i, tok):
    return x[i * tok : (i + 1) * tok]


def fold(x):
    return jnp.sum(x.reshape(x.shape[0] // 8, 8, x.shape[1]), axis=0)


def stack_heads(tok, groups, core_ref, q, go, qgx, kc, qs, gs, lo):
    core = core_ref[0]
    ids = kc[2 * tok : 2 * tok + 1, : 2 * tok].astype(jnp.float32)
    column = jnp.broadcast_to(ids, (8, 2 * tok)).T[:, 0:1]
    before = jnp.sum(jnp.where(column < ids, 1.0, 0.0), axis=0, keepdims=True)
    first = jnp.min(ids, axis=1, keepdims=True)
    starts = jnp.where(ids == first, -1.0, WINDOW + before).astype(jnp.int32)
    lo[0:1, :] = starts[:, :tok]
    lo[1:2, :] = starts[:, tok:]
    lo[2:8, :] = jnp.broadcast_to(first.astype(jnp.int32), (6, tok))
    for g in range(groups):
        for hd in range(2):
            at = (core * groups + g) * 2 + hd
            here = pl.ds(hd * tok, tok)
            qs[g, core, here, :] = q[:, lanes_at(at)]
            gs[g, core, here, :] = go[:, lanes_at(at)]
            qs[g, 1 - core, here, :] = qgx[:tok, lanes_at(g * 2 + hd)]
            gs[g, 1 - core, here, :] = qgx[tok:, lanes_at(g * 2 + hd)]


def near_sums(tok, groups, core_ref, lo_ref, qs, gs, ka, kc, va, vc, tot, term):
    core = core_ref[0]
    lo_all = lo_ref[...]
    count = seen(lo_all, ka, tok)
    los = [first_keys(core, lo_all, count, h, tok) for h in range(2)]
    blocks = WINDOW // tok + 1

    def step(g, _):
        for h in range(2):
            near = range(h + FAR, h + blocks)
            s = dot(keys_of(core, (None, ka, kc), near, g, tok), qs[g, h], NT)
            dp = dot(keys_of(core, (None, va, vc), near, g, tok), gs[g, h], NT)
            total = jnp.zeros((8, 2 * tok), jnp.float32)
            mean = jnp.zeros((8, 2 * tok), jnp.float32)
            for jj in range(FAR, blocks):
                _, w = weights_of(cut(s, jj - FAR, tok), los[h], jj, jj == blocks - 1, tok)
                total = total + fold(w)
                mean = mean + fold(w * cut(dp, jj - FAR, tok))
            tot[g, pl.ds(8 * h, 8), :] = total
            term[g, pl.ds(8 * h, 8), :] = mean
        return 0

    lax.fori_loop(0, groups, step, 0, unroll=True)


def far_values(tok, groups, core_ref, lo_ref, qs, gs, ka, kb, wk, tot, dvb, inv):
    core = core_ref[0]
    lo_all = lo_ref[...]
    count = seen(lo_all, ka, tok) + seen(lo_all, kb, tok) + seen(lo_all, wk, tok)
    los = [first_keys(core, lo_all, count, h, tok) for h in range(2)]

    def step(g, _):
        accs = []
        for h in range(2):
            s = dot(keys_of(core, ((kb, wk), ka), range(h, h + FAR), g, tok), qs[g, h], NT)
            total = tot[g, pl.ds(8 * h, 8), :]
            ws = []
            for jj in range(FAR):
                _, w = weights_of(cut(s, jj, tok), los[h], jj, False, tok)
                total = total + fold(w)
                ws.append(w)
            one = 1.0 / jnp.sum(total, axis=0, keepdims=True)
            inv[g, pl.ds(8 * h, 8), :] = jnp.broadcast_to(one, (8, 2 * tok))
            low = jnp.concatenate([(w * one).astype(jnp.bfloat16) for w in ws[: FAR - h]], 0)
            accs.append(dot(low, gs[g, h], NN))
        spread(core, accs, 0, (dvb,), g, tok)
        return 0

    lax.fori_loop(0, groups, step, 0, unroll=True)


def spread(core, accs, start, outs, g, tok):
    first = (start, max(start, 1))
    for b in range(start, start + 2 * len(outs)):
        acc = None
        for h in range(2):
            i = b - first[h]
            if 0 <= i < accs[h].shape[0] // tok:
                piece = cut(accs[h], i, tok)
                acc = piece if acc is None else acc + piece
        out = outs[(b - start) // 2]
        out[rows_at(core, b % 2, tok), lanes_at(g)] = acc.astype(out.dtype)


def far_keys(tok, groups, core_ref, lo_ref, qs, gs, ka, kb, wk, va, vb, wv, inv, term, dkb, row):
    core = core_ref[0]
    lo_all = lo_ref[...]
    count = seen(lo_all, ka, tok) + seen(lo_all, kb, tok) + seen(lo_all, wk, tok)
    los = [first_keys(core, lo_all, count, h, tok) for h in range(2)]

    def step(g, _):
        accs = []
        for h in range(2):
            s = dot(keys_of(core, ((kb, wk), ka), range(h, h + FAR), g, tok), qs[g, h], NT)
            dp = dot(keys_of(core, ((vb, wv), va), range(h, h + FAR), g, tok), gs[g, h], NT)
            one = inv[g, pl.ds(8 * h, 1), :]
            total = term[g, pl.ds(8 * h, 8), :]
            us = []
            for jj in range(FAR):
                t, w = weights_of(cut(s, jj, tok), los[h], jj, False, tok)
                total = total + fold(w * cut(dp, jj, tok))
                us.append(w * slope(t))
            mean = one * jnp.sum(total, axis=0, keepdims=True)
            row[g, pl.ds(8 * h, 8), :] = jnp.broadcast_to(mean, (8, 2 * tok))
            low = [((us[jj] * one) * (cut(dp, jj, tok) - mean)).astype(jnp.bfloat16) for jj in range(FAR - h)]
            accs.append(dot(jnp.concatenate(low, 0), qs[g, h], NN))
        spread(core, accs, 0, (dkb,), g, tok)
        return 0

    lax.fori_loop(0, groups, step, 0, unroll=True)


def near_grads(tok, groups, core_ref, lo_ref, qs, gs, kb, wk, ka, kc, vb, wv, va, vc, inv, row,
               dva, dvc, dka, dkc, dq0, dq1, dq_s):
    core = core_ref[0]
    lo_all = lo_ref[...]
    count = seen(lo_all, ka, tok) + seen(lo_all, kb, tok) + seen(lo_all, wk, tok)
    los = [first_keys(core, lo_all, count, h, tok) for h in range(2)]
    blocks = WINDOW // tok + 1

    def step(g, _):
        dvs, dks = [], []
        for h in range(2):
            k_rows = keys_of(core, ((kb, wk), ka, kc), range(h, h + blocks), g, tok)
            v_rows = keys_of(core, ((vb, wv), va, vc), range(h, h + blocks), g, tok)
            s = dot(k_rows, qs[g, h], NT)
            dp = dot(v_rows, gs[g, h], NT)
            one = inv[g, pl.ds(8 * h, 1), :]
            mean = row[g, pl.ds(8 * h, 1), :]
            low, dlow = [], []
            for jj in range(blocks):
                t, w = weights_of(cut(s, jj, tok), los[h], jj, jj == blocks - 1, tok)
                p = w * one
                low.append(p.astype(jnp.bfloat16))
                ds = p * slope(t) * (cut(dp, jj, tok) - mean)
                dlow.append(ds.astype(jnp.bfloat16))
            dvs.append(dot(jnp.concatenate(low[FAR - h :], 0), gs[g, h], NN))
            dks.append(dot(jnp.concatenate(dlow[FAR - h :], 0), qs[g, h], NN))
            dq_t = dot(k_rows.T, jnp.concatenate(dlow, 0), NN)
            dq_s[g, lax.bitwise_xor(core, h)] = dq_t.T.astype(jnp.bfloat16)
        spread(core, dvs, FAR, (dva, dvc), g, tok)
        spread(core, dks, FAR, (dka, dkc), g, tok)
        for r, dq in enumerate((dq0, dq1)):
            for hd in range(2):
                dq[:, lanes_at(2 * g + hd)] = dq_s[g, r, hd * tok : (hd + 1) * tok, :]
        return 0

    lax.fori_loop(0, groups, step, 0, unroll=True)


def merge(tok, groups, core_ref, mine, came, out):
    out[...] = (mine[...] + came[...].astype(jnp.float32)).astype(out.dtype)


def call(body, tok, groups, args, outs, scratch=()):
    vmem = pl.BlockSpec(memory_space=pltpu.VMEM)
    return pl.pallas_call(
        functools.partial(body, tok, groups),
        in_specs=[pl.BlockSpec(memory_space=pltpu.SMEM)] + [vmem] * (len(args) - 1),
        out_specs=[vmem] * len(outs),
        out_shape=[jax.ShapeDtypeStruct(s, d) for s, d in outs],
        scratch_shapes=list(scratch),
        compiler_params=pltpu.CompilerParams(vmem_limit_bytes=VMEM_LIMIT),
        name=body.__name__,
    )(*args)


VMEM_LIMIT = 4 * 1024 * 1024


def local(queries, keys, values, grad_out, segment):
    tok = queries.shape[0]
    kv_width = keys.shape[1]
    half = kv_width // 2
    groups = half // HEAD_DIM
    q_half = queries.shape[1] // 2
    bf16, f32 = jnp.bfloat16, jnp.float32
    core = lax.rem(lax.axis_index(AXES), 2)
    core_arr = core.reshape(1).astype(jnp.int32)

    def part(x, which, width):
        return lax.dynamic_slice(x, (0, which * width), (x.shape[0], width))

    seg_own = (segment + 1).astype(bf16)[None, :]
    seg_row = jnp.pad(seg_own, ((0, SEG_ROWS - 1), (tok, half - 2 * tok)))
    own_row = jnp.pad(seg_own, ((0, SEG_ROWS - 1), (0, half - tok)))
    k_in = swap(jnp.concatenate([part(keys, 1 - core, half), seg_row], 0))
    kc = jnp.concatenate([part(keys, core, half), k_in[:tok], k_in[tok:] + own_row], 0)
    v_in = swap(part(values, 1 - core, half))
    vc = jnp.concatenate([part(values, core, half), v_in, jnp.zeros((SEG_ROWS, half), bf16)], 0)
    ka = hop(kc, 1)
    va = hop(vc, 1)
    queries, grad_out, _ = lax.optimization_barrier((queries, grad_out, v_in))
    qg_in = swap(jnp.concatenate([part(queries, 1 - core, q_half), part(grad_out, 1 - core, q_half)], 0))

    rows = ((groups, 2, 2 * tok, HEAD_DIM), bf16)
    stat = ((groups, 16, 2 * tok), f32)
    kv_f = ((2 * tok, half), f32)
    kv_b = ((2 * tok, half), bf16)
    dq_o = ((tok, q_half), bf16)

    qs, gs, lo = call(
        stack_heads, tok, groups, (core_arr, queries, grad_out, qg_in, kc),
        [rows, rows, ((8, tok), jnp.int32)])
    va, qs, gs, lo = lax.optimization_barrier((va, qs, gs, lo))
    wk = ahead(kc)
    wv = ahead(vc)
    kb = forward(ka)
    vb = forward(va)
    tot, term = call(
        near_sums, tok, groups, (core_arr, lo, qs, gs, ka, kc, va, vc), [stat, stat])
    dvb, inv = call(
        far_values, tok, groups, (core_arr, lo, qs, gs, ka, kb, wk, tot), [kv_b, stat])
    cv = hop(dvb, -1)
    dkb, row = call(
        far_keys, tok, groups, (core_arr, lo, qs, gs, ka, kb, wk, va, vb, wv, inv, term), [kv_b, stat])
    ck = hop(dkb, -1)
    dva, dvc, dka, dkc, dq0, dq1 = call(
        near_grads, tok, groups, (core_arr, lo, qs, gs, kb, wk, ka, kc, vb, wv, va, vc, inv, row),
        [kv_f, kv_f, kv_f, kv_f, dq_o, dq_o],
        [pltpu.VMEM((groups, 2, 2 * tok, HEAD_DIM), bf16)])
    (dv_out,) = call(merge, tok, groups, (core_arr, dva, cv), [kv_b])
    dv = hop(dv_out, -1)
    (dk_out,) = call(merge, tok, groups, (core_arr, dka, ck), [kv_b])
    dkc, dq1, _ = lax.optimization_barrier((dkc, dq1, dv_out))
    dk_same = hop(dk_out[:tok], -1)
    dk_cross = cross(dk_out[tok:], -1)
    def place(mine, other):
        first = jnp.where(core == 0, mine, other)
        second = jnp.where(core == 0, other, mine)
        return jnp.concatenate([first, second], 1)

    grad_q = place(dq0, swap(dq1))
    sum_v = dvc + dv.astype(f32)
    grad_v = place(sum_v[:tok].astype(bf16), swap(sum_v[tok:].astype(bf16)))
    other_k = swap(dkc[tok:])
    dk_cross, grad_v = lax.optimization_barrier((dk_cross, grad_v))
    same = (dkc[:tok] + dk_same.astype(f32)).astype(bf16)
    other = (other_k + dk_cross.astype(f32)).astype(bf16)
    grad_k = place(same, other)
    return grad_q, grad_k, grad_v


def solution(mesh):
    rows = P(AXES, None)
    return jax.shard_map(
        local,
        mesh=mesh,
        in_specs=(rows, rows, rows, rows, P(AXES)),
        out_specs=(rows, rows, rows),
        check_vma=False,
    )
```

```python
import functools

import jax
import jax.numpy as jnp
from jax import lax
from jax.experimental import pallas as pl
from jax.experimental.pallas import tpu as pltpu
from jax.sharding import PartitionSpec as P

HEAD_DIM = 128
WINDOW = 512
SOFTCAP = 50.0
SCALE = 1.0 / 12.0
LOG2E = 1.4426950408889634
AXES = ("ctx", "fsdp")
NT = (((1,), (1,)), ((), ()))
NN = (((1,), (0,)), ((), ()))
SEG_ROWS = 8
FAR = 2


def dot(a, b, dims):
    return lax.dot_general(a, b, dims, preferred_element_type=jnp.float32)


def swap(x):
    n = lax.axis_size(AXES)
    return lax.ppermute(x, AXES, [(i, i ^ 1) for i in range(n)])


def hop(x, chips):
    n = lax.axis_size(AXES)
    by = 2 * chips
    return lax.ppermute(x, AXES, [(i, i + by) for i in range(n) if 0 <= i + by < n])


def cross(x, chips):
    n = lax.axis_size(AXES)
    by = 2 * chips
    return lax.ppermute(x, AXES, [(i, (i ^ 1) + by) for i in range(n) if 0 <= i + by < n])


def forward(x):
    n, row = lax.axis_size(AXES), lax.axis_size("fsdp")
    return lax.ppermute(x, AXES, [(i, i + 2) for i in range(n) if i % row < row - 2])


def ahead(x):
    n, row = lax.axis_size(AXES), lax.axis_size("fsdp")
    return lax.ppermute(x, AXES, [(i, i + 4) for i in range(n - 4) if row - 4 <= i % row < row - 2])


def rows_at(core, half, tok):
    return pl.ds(pl.multiple_of(lax.bitwise_xor(core, half) * tok, tok), tok)


def lanes_at(g):
    return pl.ds(pl.multiple_of(g * HEAD_DIM, HEAD_DIM), HEAD_DIM)


def block_of(core, pieces, b, g, tok):
    parts = pieces[b // 2]
    at = (rows_at(core, b % 2, tok), lanes_at(g))
    return parts[0][at] + parts[1][at] if isinstance(parts, tuple) else parts[at]


def seen(lo, seg_ref, tok):
    ids = seg_ref[2 * tok : 2 * tok + 1, : 2 * tok].astype(jnp.float32)
    same = jnp.where(ids == lo[2:3, 0:1].astype(jnp.float32), 1.0, 0.0)
    return jnp.sum(same, axis=1, keepdims=True).astype(jnp.int32)


def first_keys(core, lo, count, half, tok):
    mine = jnp.where(core == half, lo[0:1], lo[1:2])
    mine = jnp.where(mine < 0, WINDOW - count, mine) - half * tok
    row = lax.broadcasted_iota(jnp.int32, (1, tok), 1)
    mine = jnp.maximum(mine, row + 1)
    return jnp.concatenate([mine, mine], 1)


def keys_of(core, pieces, blocks, g, tok):
    return jnp.concatenate([block_of(core, pieces, b, g, tok) for b in blocks], 0)


def weights_of(s, lo, jj, last, tok):
    t = jnp.tanh(s * (SCALE / SOFTCAP))
    w = jnp.exp2(t * (SOFTCAP * LOG2E))
    pos = lax.broadcasted_iota(jnp.int32, s.shape, 0)
    ok = pos >= lo - jj * tok
    if last:
        col = lax.broadcasted_iota(jnp.int32, s.shape, 1)
        ok = ok & (pos <= jnp.where(col >= tok, col - tok, col))
    return t, jnp.where(ok, w, 0.0)


def slope(t):
    return SCALE - t * t * SCALE


def cut(x, i, tok):
    return x[i * tok : (i + 1) * tok]


def fold(x):
    return jnp.sum(x.reshape(x.shape[0] // 8, 8, x.shape[1]), axis=0)


def stack_heads(tok, groups, core_ref, q, go, qgx, kc, qs, gs, lo):
    core = core_ref[0]
    ids = kc[2 * tok : 2 * tok + 1, : 2 * tok].astype(jnp.float32)
    column = jnp.broadcast_to(ids, (8, 2 * tok)).T[:, 0:1]
    before = jnp.sum(jnp.where(column < ids, 1.0, 0.0), axis=0, keepdims=True)
    first = jnp.min(ids, axis=1, keepdims=True)
    starts = jnp.where(ids == first, -1.0, WINDOW + before).astype(jnp.int32)
    lo[0:1, :] = starts[:, :tok]
    lo[1:2, :] = starts[:, tok:]
    lo[2:8, :] = jnp.broadcast_to(first.astype(jnp.int32), (6, tok))
    for g in range(groups):
        for hd in range(2):
            at = (core * groups + g) * 2 + hd
            here = pl.ds(hd * tok, tok)
            qs[g, core, here, :] = q[:, lanes_at(at)]
            gs[g, core, here, :] = go[:, lanes_at(at)]
            qs[g, 1 - core, here, :] = qgx[:tok, lanes_at(g * 2 + hd)]
            gs[g, 1 - core, here, :] = qgx[tok:, lanes_at(g * 2 + hd)]


def near_sums(tok, groups, core_ref, lo_ref, qs, gs, ka, kc, va, vc, tot, term):
    core = core_ref[0]
    lo_all = lo_ref[...]
    count = seen(lo_all, ka, tok)
    los = [first_keys(core, lo_all, count, h, tok) for h in range(2)]
    blocks = WINDOW // tok + 1

    def step(g, _):
        for h in range(2):
            near = range(h + FAR, h + blocks)
            s = dot(keys_of(core, (None, ka, kc), near, g, tok), qs[g, h], NT)
            dp = dot(keys_of(core, (None, va, vc), near, g, tok), gs[g, h], NT)
            total = jnp.zeros((8, 2 * tok), jnp.float32)
            mean = jnp.zeros((8, 2 * tok), jnp.float32)
            for jj in range(FAR, blocks):
                _, w = weights_of(cut(s, jj - FAR, tok), los[h], jj, jj == blocks - 1, tok)
                total = total + fold(w)
                mean = mean + fold(w * cut(dp, jj - FAR, tok))
            tot[g, pl.ds(8 * h, 8), :] = total
            term[g, pl.ds(8 * h, 8), :] = mean
        return 0

    lax.fori_loop(0, groups, step, 0, unroll=True)


def far_values(tok, groups, core_ref, lo_ref, qs, gs, ka, kb, wk, tot, dvb, inv):
    core = core_ref[0]
    lo_all = lo_ref[...]
    count = seen(lo_all, ka, tok) + seen(lo_all, kb, tok) + seen(lo_all, wk, tok)
    los = [first_keys(core, lo_all, count, h, tok) for h in range(2)]

    def step(g, _):
        accs = []
        for h in range(2):
            s = dot(keys_of(core, ((kb, wk), ka), range(h, h + FAR), g, tok), qs[g, h], NT)
            total = tot[g, pl.ds(8 * h, 8), :]
            ws = []
            for jj in range(FAR):
                _, w = weights_of(cut(s, jj, tok), los[h], jj, False, tok)
                total = total + fold(w)
                ws.append(w)
            one = 1.0 / jnp.sum(total, axis=0, keepdims=True)
            inv[g, pl.ds(8 * h, 8), :] = jnp.broadcast_to(one, (8, 2 * tok))
            low = jnp.concatenate([(w * one).astype(jnp.bfloat16) for w in ws[: FAR - h]], 0)
            accs.append(dot(low, gs[g, h], NN))
        spread(core, accs, 0, (dvb,), g, tok)
        return 0

    lax.fori_loop(0, groups, step, 0, unroll=True)


def spread(core, accs, start, outs, g, tok):
    first = (start, max(start, 1))
    for b in range(start, start + 2 * len(outs)):
        acc = None
        for h in range(2):
            i = b - first[h]
            if 0 <= i < accs[h].shape[0] // tok:
                piece = cut(accs[h], i, tok)
                acc = piece if acc is None else acc + piece
        out = outs[(b - start) // 2]
        out[rows_at(core, b % 2, tok), lanes_at(g)] = acc.astype(out.dtype)


def far_keys(tok, groups, core_ref, lo_ref, qs, gs, ka, kb, wk, va, vb, wv, inv, term, dkb, row):
    core = core_ref[0]
    lo_all = lo_ref[...]
    count = seen(lo_all, ka, tok) + seen(lo_all, kb, tok) + seen(lo_all, wk, tok)
    los = [first_keys(core, lo_all, count, h, tok) for h in range(2)]

    def step(g, _):
        accs = []
        for h in range(2):
            s = dot(keys_of(core, ((kb, wk), ka), range(h, h + FAR), g, tok), qs[g, h], NT)
            dp = dot(keys_of(core, ((vb, wv), va), range(h, h + FAR), g, tok), gs[g, h], NT)
            one = inv[g, pl.ds(8 * h, 1), :]
            total = term[g, pl.ds(8 * h, 8), :]
            us = []
            for jj in range(FAR):
                t, w = weights_of(cut(s, jj, tok), los[h], jj, False, tok)
                total = total + fold(w * cut(dp, jj, tok))
                us.append(w * slope(t))
            mean = one * jnp.sum(total, axis=0, keepdims=True)
            row[g, pl.ds(8 * h, 8), :] = jnp.broadcast_to(mean, (8, 2 * tok))
            low = [((us[jj] * one) * (cut(dp, jj, tok) - mean)).astype(jnp.bfloat16) for jj in range(FAR - h)]
            accs.append(dot(jnp.concatenate(low, 0), qs[g, h], NN))
        spread(core, accs, 0, (dkb,), g, tok)
        return 0

    lax.fori_loop(0, groups, step, 0, unroll=True)


def near_grads(tok, groups, core_ref, lo_ref, qs, gs, kb, wk, ka, kc, vb, wv, va, vc, inv, row,
               dva, dvc, dka, dkc, dq0, dq1, dq_s):
    core = core_ref[0]
    lo_all = lo_ref[...]
    count = seen(lo_all, ka, tok) + seen(lo_all, kb, tok) + seen(lo_all, wk, tok)
    los = [first_keys(core, lo_all, count, h, tok) for h in range(2)]
    blocks = WINDOW // tok + 1

    def step(g, _):
        dvs, dks = [], []
        for h in range(2):
            k_rows = keys_of(core, ((kb, wk), ka, kc), range(h, h + blocks), g, tok)
            v_rows = keys_of(core, ((vb, wv), va, vc), range(h, h + blocks), g, tok)
            s = dot(k_rows, qs[g, h], NT)
            dp = dot(v_rows, gs[g, h], NT)
            one = inv[g, pl.ds(8 * h, 1), :]
            mean = row[g, pl.ds(8 * h, 1), :]
            low, dlow = [], []
            for jj in range(blocks):
                t, w = weights_of(cut(s, jj, tok), los[h], jj, jj == blocks - 1, tok)
                p = w * one
                low.append(p.astype(jnp.bfloat16))
                ds = p * slope(t) * (cut(dp, jj, tok) - mean)
                dlow.append(ds.astype(jnp.bfloat16))
            dvs.append(dot(jnp.concatenate(low[FAR - h :], 0), gs[g, h], NN))
            dks.append(dot(jnp.concatenate(dlow[FAR - h :], 0), qs[g, h], NN))
            dq_t = dot(k_rows.T, jnp.concatenate(dlow, 0), NN)
            dq_s[g, lax.bitwise_xor(core, h)] = dq_t.T.astype(jnp.bfloat16)
        spread(core, dvs, FAR, (dva, dvc), g, tok)
        spread(core, dks, FAR, (dka, dkc), g, tok)
        for r, dq in enumerate((dq0, dq1)):
            for hd in range(2):
                dq[:, lanes_at(2 * g + hd)] = dq_s[g, r, hd * tok : (hd + 1) * tok, :]
        return 0

    lax.fori_loop(0, groups, step, 0, unroll=True)


def merge(tok, groups, core_ref, mine, came, out):
    out[...] = (mine[...] + came[...].astype(jnp.float32)).astype(out.dtype)


def call(body, tok, groups, args, outs, scratch=()):
    vmem = pl.BlockSpec(memory_space=pltpu.VMEM)
    return pl.pallas_call(
        functools.partial(body, tok, groups),
        in_specs=[pl.BlockSpec(memory_space=pltpu.SMEM)] + [vmem] * (len(args) - 1),
        out_specs=[vmem] * len(outs),
        out_shape=[jax.ShapeDtypeStruct(s, d) for s, d in outs],
        scratch_shapes=list(scratch),
        compiler_params=pltpu.CompilerParams(vmem_limit_bytes=VMEM_LIMIT),
        name=body.__name__,
    )(*args)


VMEM_LIMIT = 4 * 1024 * 1024


def local(queries, keys, values, grad_out, segment):
    tok = queries.shape[0]
    kv_width = keys.shape[1]
    half = kv_width // 2
    groups = half // HEAD_DIM
    q_half = queries.shape[1] // 2
    bf16, f32 = jnp.bfloat16, jnp.float32
    core = lax.rem(lax.axis_index(AXES), 2)
    core_arr = core.reshape(1).astype(jnp.int32)

    def part(x, which, width):
        return lax.dynamic_slice(x, (0, which * width), (x.shape[0], width))

    seg_own = (segment + 1).astype(bf16)[None, :]
    seg_row = jnp.pad(seg_own, ((0, SEG_ROWS - 1), (tok, half - 2 * tok)))
    own_row = jnp.pad(seg_own, ((0, SEG_ROWS - 1), (0, half - tok)))
    k_in = swap(jnp.concatenate([part(keys, 1 - core, half), seg_row], 0))
    kc = jnp.concatenate([part(keys, core, half), k_in[:tok], k_in[tok:] + own_row], 0)
    v_in = swap(part(values, 1 - core, half))
    vc = jnp.concatenate([part(values, core, half), v_in, jnp.zeros((SEG_ROWS, half), bf16)], 0)
    ka = hop(kc, 1)
    va = hop(vc, 1)
    queries, grad_out, _ = lax.optimization_barrier((queries, grad_out, v_in))
    qg_in = swap(jnp.concatenate([part(queries, 1 - core, q_half), part(grad_out, 1 - core, q_half)], 0))

    rows = ((groups, 2, 2 * tok, HEAD_DIM), bf16)
    stat = ((groups, 16, 2 * tok), f32)
    kv_f = ((2 * tok, half), f32)
    kv_b = ((2 * tok, half), bf16)
    dq_o = ((tok, q_half), bf16)

    qs, gs, lo = call(
        stack_heads, tok, groups, (core_arr, queries, grad_out, qg_in, kc),
        [rows, rows, ((8, tok), jnp.int32)])
    va, qs, gs, lo = lax.optimization_barrier((va, qs, gs, lo))
    wk = ahead(kc)
    wv = ahead(vc)
    kb = forward(ka)
    vb = forward(va)
    tot, term = call(
        near_sums, tok, groups, (core_arr, lo, qs, gs, ka, kc, va, vc), [stat, stat])
    dvb, inv = call(
        far_values, tok, groups, (core_arr, lo, qs, gs, ka, kb, wk, tot), [kv_b, stat])
    cv = hop(dvb, -1)
    dkb, row = call(
        far_keys, tok, groups, (core_arr, lo, qs, gs, ka, kb, wk, va, vb, wv, inv, term), [kv_b, stat])
    ck = hop(dkb, -1)
    dva, dvc, dka, dkc, dq0, dq1 = call(
        near_grads, tok, groups, (core_arr, lo, qs, gs, kb, wk, ka, kc, vb, wv, va, vc, inv, row),
        [kv_f, kv_f, kv_f, kv_f, dq_o, dq_o],
        [pltpu.VMEM((groups, 2, 2 * tok, HEAD_DIM), bf16)])
    (dv_out,) = call(merge, tok, groups, (core_arr, dva, cv), [kv_b])
    dv = hop(dv_out, -1)
    (dk_out,) = call(merge, tok, groups, (core_arr, dka, ck), [kv_b])
    dkc, dq1, _ = lax.optimization_barrier((dkc, dq1, dv_out))
    dk_same = hop(dk_out[:tok], -1)
    dk_cross = cross(dk_out[tok:], -1)
    def place(mine, other):
        first = jnp.where(core == 0, mine, other)
        second = jnp.where(core == 0, other, mine)
        return jnp.concatenate([first, second], 1)

    grad_q = place(dq0, swap(dq1))
    sum_v = dvc + dv.astype(f32)
    grad_v = place(sum_v[:tok].astype(bf16), swap(sum_v[tok:].astype(bf16)))
    other_k = swap(dkc[tok:])
    dk_cross, grad_v = lax.optimization_barrier((dk_cross, grad_v))
    same = (dkc[:tok] + dk_same.astype(f32)).astype(bf16)
    other = (other_k + dk_cross.astype(f32)).astype(bf16)
    grad_k = place(same, other)
    return grad_q, grad_k, grad_v


def solution(mesh):
    rows = P(AXES, None)
    return jax.shard_map(
        local,
        mesh=mesh,
        in_specs=(rows, rows, rows, rows, P(AXES)),
        out_specs=(rows, rows, rows),
        check_vma=False,
    )
```

```python
import functools

import jax
import jax.numpy as jnp
from jax import lax
from jax.experimental import pallas as pl
from jax.experimental.pallas import tpu as pltpu
from jax.sharding import PartitionSpec as P

HEAD_DIM = 128
WINDOW = 512
SOFTCAP = 50.0
SCALE = 1.0 / 12.0
LOG2E = 1.4426950408889634
AXES = ("ctx", "fsdp")
NT = (((1,), (1,)), ((), ()))
NN = (((1,), (0,)), ((), ()))
SEG_ROWS = 8
FAR = 2


def dot(a, b, dims):
    return lax.dot_general(a, b, dims, preferred_element_type=jnp.float32)


def swap(x):
    n = lax.axis_size(AXES)
    return lax.ppermute(x, AXES, [(i, i ^ 1) for i in range(n)])


def hop(x, chips):
    n = lax.axis_size(AXES)
    by = 2 * chips
    return lax.ppermute(x, AXES, [(i, i + by) for i in range(n) if 0 <= i + by < n])


def cross(x, chips):
    n = lax.axis_size(AXES)
    by = 2 * chips
    return lax.ppermute(x, AXES, [(i, (i ^ 1) + by) for i in range(n) if 0 <= i + by < n])


def forward(x):
    n, row = lax.axis_size(AXES), lax.axis_size("fsdp")
    return lax.ppermute(x, AXES, [(i, i + 2) for i in range(n) if i % row < row - 2])


def ahead(x):
    n, row = lax.axis_size(AXES), lax.axis_size("fsdp")
    return lax.ppermute(x, AXES, [(i, i + 4) for i in range(n - 4) if row - 4 <= i % row < row - 2])


def rows_at(core, half, tok):
    return pl.ds(pl.multiple_of(lax.bitwise_xor(core, half) * tok, tok), tok)


def lanes_at(g):
    return pl.ds(pl.multiple_of(g * HEAD_DIM, HEAD_DIM), HEAD_DIM)


def block_of(core, pieces, b, g, tok):
    parts = pieces[b // 2]
    at = (rows_at(core, b % 2, tok), lanes_at(g))
    return parts[0][at] + parts[1][at] if isinstance(parts, tuple) else parts[at]


def seen(lo, seg_ref, tok):
    ids = seg_ref[2 * tok : 2 * tok + 1, : 2 * tok].astype(jnp.float32)
    same = jnp.where(ids == lo[2:3, 0:1].astype(jnp.float32), 1.0, 0.0)
    return jnp.sum(same, axis=1, keepdims=True).astype(jnp.int32)


def first_keys(core, lo, count, half, tok):
    mine = jnp.where(core == half, lo[0:1], lo[1:2])
    mine = jnp.where(mine < 0, WINDOW - count, mine) - half * tok
    row = lax.broadcasted_iota(jnp.int32, (1, tok), 1)
    mine = jnp.maximum(mine, row + 1)
    return jnp.concatenate([mine, mine], 1)


def keys_of(core, pieces, blocks, g, tok):
    return jnp.concatenate([block_of(core, pieces, b, g, tok) for b in blocks], 0)


def weights_of(s, lo, jj, last, tok):
    t = jnp.tanh(s * (SCALE / SOFTCAP))
    w = jnp.exp2(t * (SOFTCAP * LOG2E))
    pos = lax.broadcasted_iota(jnp.int32, s.shape, 0)
    ok = pos >= lo - jj * tok
    if last:
        col = lax.broadcasted_iota(jnp.int32, s.shape, 1)
        ok = ok & (pos <= jnp.where(col >= tok, col - tok, col))
    return t, jnp.where(ok, w, 0.0)


def slope(t):
    return SCALE - t * t * SCALE


def cut(x, i, tok):
    return x[i * tok : (i + 1) * tok]


def fold(x):
    return jnp.sum(x.reshape(x.shape[0] // 8, 8, x.shape[1]), axis=0)


def stack_heads(tok, groups, core_ref, q, go, qgx, kc, qs, gs, lo):
    core = core_ref[0]
    ids = kc[2 * tok : 2 * tok + 1, : 2 * tok].astype(jnp.float32)
    column = jnp.broadcast_to(ids, (8, 2 * tok)).T[:, 0:1]
    before = jnp.sum(jnp.where(column < ids, 1.0, 0.0), axis=0, keepdims=True)
    first = jnp.min(ids, axis=1, keepdims=True)
    starts = jnp.where(ids == first, -1.0, WINDOW + before).astype(jnp.int32)
    lo[0:1, :] = starts[:, :tok]
    lo[1:2, :] = starts[:, tok:]
    lo[2:8, :] = jnp.broadcast_to(first.astype(jnp.int32), (6, tok))
    for g in range(groups):
        for hd in range(2):
            at = (core * groups + g) * 2 + hd
            here = pl.ds(hd * tok, tok)
            qs[g, core, here, :] = q[:, lanes_at(at)]
            gs[g, core, here, :] = go[:, lanes_at(at)]
            qs[g, 1 - core, here, :] = qgx[:tok, lanes_at(g * 2 + hd)]
            gs[g, 1 - core, here, :] = qgx[tok:, lanes_at(g * 2 + hd)]


def near_sums(tok, groups, core_ref, lo_ref, qs, gs, ka, kc, va, vc, tot, term):
    core = core_ref[0]
    lo_all = lo_ref[...]
    count = seen(lo_all, ka, tok)
    los = [first_keys(core, lo_all, count, h, tok) for h in range(2)]
    blocks = WINDOW // tok + 1

    def step(g, _):
        for h in range(2):
            near = range(h + FAR, h + blocks)
            s = dot(keys_of(core, (None, ka, kc), near, g, tok), qs[g, h], NT)
            dp = dot(keys_of(core, (None, va, vc), near, g, tok), gs[g, h], NT)
            total = jnp.zeros((8, 2 * tok), jnp.float32)
            mean = jnp.zeros((8, 2 * tok), jnp.float32)
            for jj in range(FAR, blocks):
                _, w = weights_of(cut(s, jj - FAR, tok), los[h], jj, jj == blocks - 1, tok)
                total = total + fold(w)
                mean = mean + fold(w * cut(dp, jj - FAR, tok))
            tot[g, pl.ds(8 * h, 8), :] = total
            term[g, pl.ds(8 * h, 8), :] = mean
        return 0

    lax.fori_loop(0, groups, step, 0, unroll=True)


def in_turn(groups, products, weigh, finish):
    units = [(g, h) for g in range(groups) for h in range(2)]
    ready, waiting = products(*units[0]), None
    for i, (g, h) in enumerate(units):
        ahead_of = products(*units[i + 1]) if i + 1 < len(units) else None
        held = weigh(g, h, ready)
        if waiting is not None:
            finish(*waiting)
        ready, waiting = ahead_of, (g, h, held)
    finish(*waiting)


def far_values(tok, groups, core_ref, lo_ref, qs, gs, ka, kb, wk, tot, dvb, inv):
    core = core_ref[0]
    lo_all = lo_ref[...]
    count = seen(lo_all, ka, tok) + seen(lo_all, kb, tok) + seen(lo_all, wk, tok)
    los = [first_keys(core, lo_all, count, h, tok) for h in range(2)]
    accs = {}

    def products(g, h):
        return dot(keys_of(core, ((kb, wk), ka), range(h, h + FAR), g, tok), qs[g, h], NT)

    def weigh(g, h, s):
        total = tot[g, pl.ds(8 * h, 8), :]
        ws = []
        for jj in range(FAR):
            _, w = weights_of(cut(s, jj, tok), los[h], jj, False, tok)
            total = total + fold(w)
            ws.append(w)
        return total, ws

    def finish(g, h, held):
        total, ws = held
        one = 1.0 / jnp.sum(total, axis=0, keepdims=True)
        inv[g, pl.ds(8 * h, 8), :] = jnp.broadcast_to(one, (8, 2 * tok))
        low = jnp.concatenate([(w * one).astype(jnp.bfloat16) for w in ws[: FAR - h]], 0)
        accs[h] = dot(low, gs[g, h], NN)
        if h == 1:
            spread(core, accs, 0, (dvb,), g, tok)

    in_turn(groups, products, weigh, finish)


def spread(core, accs, start, outs, g, tok):
    first = (start, max(start, 1))
    for b in range(start, start + 2 * len(outs)):
        acc = None
        for h in range(2):
            i = b - first[h]
            if 0 <= i < accs[h].shape[0] // tok:
                piece = cut(accs[h], i, tok)
                acc = piece if acc is None else acc + piece
        out = outs[(b - start) // 2]
        out[rows_at(core, b % 2, tok), lanes_at(g)] = acc.astype(out.dtype)


def far_keys(tok, groups, core_ref, lo_ref, qs, gs, ka, kb, wk, va, vb, wv, inv, term, dkb, row):
    core = core_ref[0]
    lo_all = lo_ref[...]
    count = seen(lo_all, ka, tok) + seen(lo_all, kb, tok) + seen(lo_all, wk, tok)
    los = [first_keys(core, lo_all, count, h, tok) for h in range(2)]
    accs = {}

    def products(g, h):
        blocks = range(h, h + FAR)
        return (
            dot(keys_of(core, ((kb, wk), ka), blocks, g, tok), qs[g, h], NT),
            dot(keys_of(core, ((vb, wv), va), blocks, g, tok), gs[g, h], NT),
        )

    def weigh(g, h, ready):
        s, dp = ready
        total = term[g, pl.ds(8 * h, 8), :]
        us = []
        for jj in range(FAR):
            t, w = weights_of(cut(s, jj, tok), los[h], jj, False, tok)
            total = total + fold(w * cut(dp, jj, tok))
            us.append(w * slope(t))
        return total, us, dp

    def finish(g, h, held):
        total, us, dp = held
        one = inv[g, pl.ds(8 * h, 1), :]
        mean = one * jnp.sum(total, axis=0, keepdims=True)
        row[g, pl.ds(8 * h, 8), :] = jnp.broadcast_to(mean, (8, 2 * tok))
        low = [((us[jj] * one) * (cut(dp, jj, tok) - mean)).astype(jnp.bfloat16) for jj in range(FAR - h)]
        accs[h] = dot(jnp.concatenate(low, 0), qs[g, h], NN)
        if h == 1:
            spread(core, accs, 0, (dkb,), g, tok)

    in_turn(groups, products, weigh, finish)


def near_grads(tok, groups, core_ref, lo_ref, qs, gs, kb, wk, ka, kc, vb, wv, va, vc, inv, row,
               dva, dvc, dka, dkc, dq0, dq1, dq_s):
    core = core_ref[0]
    lo_all = lo_ref[...]
    count = seen(lo_all, ka, tok) + seen(lo_all, kb, tok) + seen(lo_all, wk, tok)
    los = [first_keys(core, lo_all, count, h, tok) for h in range(2)]
    blocks = WINDOW // tok + 1

    def step(g, _):
        dvs, dks = [], []
        for h in range(2):
            k_rows = keys_of(core, ((kb, wk), ka, kc), range(h, h + blocks), g, tok)
            v_rows = keys_of(core, ((vb, wv), va, vc), range(h, h + blocks), g, tok)
            s = dot(k_rows, qs[g, h], NT)
            dp = dot(v_rows, gs[g, h], NT)
            one = inv[g, pl.ds(8 * h, 1), :]
            mean = row[g, pl.ds(8 * h, 1), :]
            low, dlow = [], []
            for jj in range(blocks):
                t, w = weights_of(cut(s, jj, tok), los[h], jj, jj == blocks - 1, tok)
                p = w * one
                low.append(p.astype(jnp.bfloat16))
                ds = p * slope(t) * (cut(dp, jj, tok) - mean)
                dlow.append(ds.astype(jnp.bfloat16))
            dvs.append(dot(jnp.concatenate(low[FAR - h :], 0), gs[g, h], NN))
            dks.append(dot(jnp.concatenate(dlow[FAR - h :], 0), qs[g, h], NN))
            dq_t = dot(k_rows.T, jnp.concatenate(dlow, 0), NN)
            dq_s[g, lax.bitwise_xor(core, h)] = dq_t.T.astype(jnp.bfloat16)
        spread(core, dvs, FAR, (dva, dvc), g, tok)
        spread(core, dks, FAR, (dka, dkc), g, tok)
        for r, dq in enumerate((dq0, dq1)):
            for hd in range(2):
                dq[:, lanes_at(2 * g + hd)] = dq_s[g, r, hd * tok : (hd + 1) * tok, :]
        return 0

    lax.fori_loop(0, groups, step, 0, unroll=True)


def merge(tok, groups, core_ref, mine, came, out):
    out[...] = (mine[...] + came[...].astype(jnp.float32)).astype(out.dtype)


def call(body, tok, groups, args, outs, scratch=()):
    vmem = pl.BlockSpec(memory_space=pltpu.VMEM)
    return pl.pallas_call(
        functools.partial(body, tok, groups),
        in_specs=[pl.BlockSpec(memory_space=pltpu.SMEM)] + [vmem] * (len(args) - 1),
        out_specs=[vmem] * len(outs),
        out_shape=[jax.ShapeDtypeStruct(s, d) for s, d in outs],
        scratch_shapes=list(scratch),
        compiler_params=pltpu.CompilerParams(vmem_limit_bytes=VMEM_LIMIT),
        name=body.__name__,
    )(*args)


VMEM_LIMIT = 16 * 1024 * 1024


def local(queries, keys, values, grad_out, segment):
    tok = queries.shape[0]
    kv_width = keys.shape[1]
    half = kv_width // 2
    groups = half // HEAD_DIM
    q_half = queries.shape[1] // 2
    bf16, f32 = jnp.bfloat16, jnp.float32
    core = lax.rem(lax.axis_index(AXES), 2)
    core_arr = core.reshape(1).astype(jnp.int32)

    def part(x, which, width):
        return lax.dynamic_slice(x, (0, which * width), (x.shape[0], width))

    seg_own = (segment + 1).astype(bf16)[None, :]
    seg_row = jnp.pad(seg_own, ((0, SEG_ROWS - 1), (tok, half - 2 * tok)))
    own_row = jnp.pad(seg_own, ((0, SEG_ROWS - 1), (0, half - tok)))
    k_in = swap(jnp.concatenate([part(keys, 1 - core, half), seg_row], 0))
    kc = jnp.concatenate([part(keys, core, half), k_in[:tok], k_in[tok:] + own_row], 0)
    v_in = swap(part(values, 1 - core, half))
    vc = jnp.concatenate([part(values, core, half), v_in, jnp.zeros((SEG_ROWS, half), bf16)], 0)
    ka = hop(kc, 1)
    va = hop(vc, 1)
    queries, grad_out, _ = lax.optimization_barrier((queries, grad_out, v_in))
    qg_in = swap(jnp.concatenate([part(queries, 1 - core, q_half), part(grad_out, 1 - core, q_half)], 0))

    rows = ((groups, 2, 2 * tok, HEAD_DIM), bf16)
    stat = ((groups, 16, 2 * tok), f32)
    kv_f = ((2 * tok, half), f32)
    kv_b = ((2 * tok, half), bf16)
    dq_o = ((tok, q_half), bf16)

    qs, gs, lo = call(
        stack_heads, tok, groups, (core_arr, queries, grad_out, qg_in, kc),
        [rows, rows, ((8, tok), jnp.int32)])
    va, qs, gs, lo = lax.optimization_barrier((va, qs, gs, lo))
    wk = ahead(kc)
    wv = ahead(vc)
    kb = forward(ka)
    vb = forward(va)
    tot, term = call(
        near_sums, tok, groups, (core_arr, lo, qs, gs, ka, kc, va, vc), [stat, stat])
    dvb, inv = call(
        far_values, tok, groups, (core_arr, lo, qs, gs, ka, kb, wk, tot), [kv_b, stat])
    cv = hop(dvb, -1)
    dkb, row = call(
        far_keys, tok, groups, (core_arr, lo, qs, gs, ka, kb, wk, va, vb, wv, inv, term), [kv_b, stat])
    ck = hop(dkb, -1)
    dva, dvc, dka, dkc, dq0, dq1 = call(
        near_grads, tok, groups, (core_arr, lo, qs, gs, kb, wk, ka, kc, vb, wv, va, vc, inv, row),
        [kv_f, kv_f, kv_f, kv_f, dq_o, dq_o],
        [pltpu.VMEM((groups, 2, 2 * tok, HEAD_DIM), bf16)])
    (dv_out,) = call(merge, tok, groups, (core_arr, dva, cv), [kv_b])
    dv = hop(dv_out, -1)
    (dk_out,) = call(merge, tok, groups, (core_arr, dka, ck), [kv_b])
    dkc, dq1, _ = lax.optimization_barrier((dkc, dq1, dv_out))
    dk_same = hop(dk_out[:tok], -1)
    dk_cross = cross(dk_out[tok:], -1)
    def place(mine, other):
        first = jnp.where(core == 0, mine, other)
        second = jnp.where(core == 0, other, mine)
        return jnp.concatenate([first, second], 1)

    grad_q = place(dq0, swap(dq1))
    sum_v = dvc + dv.astype(f32)
    grad_v = place(sum_v[:tok].astype(bf16), swap(sum_v[tok:].astype(bf16)))
    other_k = swap(dkc[tok:])
    dk_cross, grad_v = lax.optimization_barrier((dk_cross, grad_v))
    same = (dkc[:tok] + dk_same.astype(f32)).astype(bf16)
    other = (other_k + dk_cross.astype(f32)).astype(bf16)
    grad_k = place(same, other)
    return grad_q, grad_k, grad_v


def solution(mesh):
    rows = P(AXES, None)
    return jax.shard_map(
        local,
        mesh=mesh,
        in_specs=(rows, rows, rows, rows, P(AXES)),
        out_specs=(rows, rows, rows),
        check_vma=False,
    )
```

```python
import functools

import jax
import jax.numpy as jnp
from jax import lax
from jax.experimental import pallas as pl
from jax.experimental.pallas import tpu as pltpu
from jax.sharding import PartitionSpec as P

HEAD_DIM = 128
WINDOW = 512
SOFTCAP = 50.0
SCALE = 1.0 / 12.0
LOG2E = 1.4426950408889634
AXES = ("ctx", "fsdp")
NT = (((1,), (1,)), ((), ()))
NN = (((1,), (0,)), ((), ()))
SEG_ROWS = 8
FAR = 2


def dot(a, b, dims):
    return lax.dot_general(a, b, dims, preferred_element_type=jnp.float32)


def swap(x):
    n = lax.axis_size(AXES)
    return lax.ppermute(x, AXES, [(i, i ^ 1) for i in range(n)])


def hop(x, chips):
    n = lax.axis_size(AXES)
    by = 2 * chips
    return lax.ppermute(x, AXES, [(i, i + by) for i in range(n) if 0 <= i + by < n])


def cross(x, chips):
    n = lax.axis_size(AXES)
    by = 2 * chips
    return lax.ppermute(x, AXES, [(i, (i ^ 1) + by) for i in range(n) if 0 <= i + by < n])


def forward(x):
    n, row = lax.axis_size(AXES), lax.axis_size("fsdp")
    return lax.ppermute(x, AXES, [(i, i + 2) for i in range(n) if i % row < row - 2])


def ahead(x):
    n, row = lax.axis_size(AXES), lax.axis_size("fsdp")
    return lax.ppermute(x, AXES, [(i, i + 4) for i in range(n - 4) if row - 4 <= i % row < row - 2])


def rows_at(core, half, tok):
    return pl.ds(pl.multiple_of(lax.bitwise_xor(core, half) * tok, tok), tok)


def lanes_at(g):
    return pl.ds(pl.multiple_of(g * HEAD_DIM, HEAD_DIM), HEAD_DIM)


def block_of(core, pieces, b, g, tok):
    parts = pieces[b // 2]
    at = (rows_at(core, b % 2, tok), lanes_at(g))
    return parts[0][at] + parts[1][at] if isinstance(parts, tuple) else parts[at]


def seen(lo, seg_ref, tok):
    ids = seg_ref[2 * tok : 2 * tok + 1, : 2 * tok].astype(jnp.float32)
    same = jnp.where(ids == lo[2:3, 0:1].astype(jnp.float32), 1.0, 0.0)
    return jnp.sum(same, axis=1, keepdims=True).astype(jnp.int32)


def first_keys(core, lo, count, half, tok):
    mine = jnp.where(core == half, lo[0:1], lo[1:2])
    mine = jnp.where(mine < 0, WINDOW - count, mine) - half * tok
    row = lax.broadcasted_iota(jnp.int32, (1, tok), 1)
    mine = jnp.maximum(mine, row + 1)
    return jnp.concatenate([mine, mine], 1)


def keys_of(core, pieces, blocks, g, tok):
    return jnp.concatenate([block_of(core, pieces, b, g, tok) for b in blocks], 0)


def weights_of(s, lo, jj, last, tok):
    t = jnp.tanh(s * (SCALE / SOFTCAP))
    w = jnp.exp2(t * (SOFTCAP * LOG2E))
    pos = lax.broadcasted_iota(jnp.int32, s.shape, 0)
    ok = pos >= lo - jj * tok
    if last:
        col = lax.broadcasted_iota(jnp.int32, s.shape, 1)
        ok = ok & (pos <= jnp.where(col >= tok, col - tok, col))
    return t, jnp.where(ok, w, 0.0)


def slope(t):
    return SCALE - t * t * SCALE


def cut(x, i, tok):
    return x[i * tok : (i + 1) * tok]


def fold(x):
    return jnp.sum(x.reshape(x.shape[0] // 8, 8, x.shape[1]), axis=0)


def stack_heads(tok, groups, core_ref, q, go, qgx, kc, qs, gs, lo):
    core = core_ref[0]
    ids = kc[2 * tok : 2 * tok + 1, : 2 * tok].astype(jnp.float32)
    column = jnp.broadcast_to(ids, (8, 2 * tok)).T[:, 0:1]
    before = jnp.sum(jnp.where(column < ids, 1.0, 0.0), axis=0, keepdims=True)
    first = jnp.min(ids, axis=1, keepdims=True)
    starts = jnp.where(ids == first, -1.0, WINDOW + before).astype(jnp.int32)
    lo[0:1, :] = starts[:, :tok]
    lo[1:2, :] = starts[:, tok:]
    lo[2:8, :] = jnp.broadcast_to(first.astype(jnp.int32), (6, tok))
    for g in range(groups):
        for hd in range(2):
            at = (core * groups + g) * 2 + hd
            here = pl.ds(hd * tok, tok)
            qs[g, core, here, :] = q[:, lanes_at(at)]
            gs[g, core, here, :] = go[:, lanes_at(at)]
            qs[g, 1 - core, here, :] = qgx[:tok, lanes_at(g * 2 + hd)]
            gs[g, 1 - core, here, :] = qgx[tok:, lanes_at(g * 2 + hd)]


def near_sums(tok, groups, core_ref, lo_ref, qs, gs, ka, kc, va, vc, tot, term):
    core = core_ref[0]
    lo_all = lo_ref[...]
    count = seen(lo_all, ka, tok)
    los = [first_keys(core, lo_all, count, h, tok) for h in range(2)]
    blocks = WINDOW // tok + 1

    def step(g, _):
        for h in range(2):
            near = range(h + FAR, h + blocks)
            s = dot(keys_of(core, (None, ka, kc), near, g, tok), qs[g, h], NT)
            dp = dot(keys_of(core, (None, va, vc), near, g, tok), gs[g, h], NT)
            total = jnp.zeros((8, 2 * tok), jnp.float32)
            mean = jnp.zeros((8, 2 * tok), jnp.float32)
            for jj in range(FAR, blocks):
                _, w = weights_of(cut(s, jj - FAR, tok), los[h], jj, jj == blocks - 1, tok)
                total = total + fold(w)
                mean = mean + fold(w * cut(dp, jj - FAR, tok))
            tot[g, pl.ds(8 * h, 8), :] = total
            term[g, pl.ds(8 * h, 8), :] = mean
        return 0

    lax.fori_loop(0, groups, step, 0, unroll=True)


def in_turn(groups, products, weigh, finish):
    units = [(g, h) for g in range(groups) for h in range(2)]
    ready, waiting = products(*units[0]), None
    for i, (g, h) in enumerate(units):
        ahead_of = products(*units[i + 1]) if i + 1 < len(units) else None
        held = weigh(g, h, ready)
        if waiting is not None:
            finish(*waiting)
        ready, waiting = ahead_of, (g, h, held)
    finish(*waiting)


def far_values(tok, groups, core_ref, lo_ref, qs, gs, ka, kb, wk, tot, dvb, inv):
    core = core_ref[0]
    lo_all = lo_ref[...]
    count = seen(lo_all, ka, tok) + seen(lo_all, kb, tok) + seen(lo_all, wk, tok)
    los = [first_keys(core, lo_all, count, h, tok) for h in range(2)]
    accs = {}

    def products(g, h):
        return dot(keys_of(core, ((kb, wk), ka), range(h, h + FAR), g, tok), qs[g, h], NT)

    def weigh(g, h, s):
        total = tot[g, pl.ds(8 * h, 8), :]
        ws = []
        for jj in range(FAR):
            _, w = weights_of(cut(s, jj, tok), los[h], jj, False, tok)
            total = total + fold(w)
            ws.append(w)
        return total, ws

    def finish(g, h, held):
        total, ws = held
        one = 1.0 / jnp.sum(total, axis=0, keepdims=True)
        inv[g, pl.ds(8 * h, 8), :] = jnp.broadcast_to(one, (8, 2 * tok))
        low = jnp.concatenate([(w * one).astype(jnp.bfloat16) for w in ws[: FAR - h]], 0)
        accs[h] = dot(low, gs[g, h], NN)
        if h == 1:
            spread(core, accs, 0, (dvb,), g, tok)

    in_turn(groups, products, weigh, finish)


def spread(core, accs, start, outs, g, tok):
    first = (start, max(start, 1))
    for b in range(start, start + 2 * len(outs)):
        acc = None
        for h in range(2):
            i = b - first[h]
            if 0 <= i < accs[h].shape[0] // tok:
                piece = cut(accs[h], i, tok)
                acc = piece if acc is None else acc + piece
        out = outs[(b - start) // 2]
        out[rows_at(core, b % 2, tok), lanes_at(g)] = acc.astype(out.dtype)


def far_keys(tok, groups, core_ref, lo_ref, qs, gs, ka, kb, wk, va, vb, wv, inv, term, dkb, row):
    core = core_ref[0]
    lo_all = lo_ref[...]
    count = seen(lo_all, ka, tok) + seen(lo_all, kb, tok) + seen(lo_all, wk, tok)
    los = [first_keys(core, lo_all, count, h, tok) for h in range(2)]
    accs = {}

    def products(g, h):
        blocks = range(h, h + FAR)
        return (
            dot(keys_of(core, ((kb, wk), ka), blocks, g, tok), qs[g, h], NT),
            dot(keys_of(core, ((vb, wv), va), blocks, g, tok), gs[g, h], NT),
        )

    def weigh(g, h, ready):
        s, dp = ready
        total = term[g, pl.ds(8 * h, 8), :]
        us = []
        for jj in range(FAR):
            t, w = weights_of(cut(s, jj, tok), los[h], jj, False, tok)
            total = total + fold(w * cut(dp, jj, tok))
            us.append(w * slope(t))
        return total, us, dp

    def finish(g, h, held):
        total, us, dp = held
        one = inv[g, pl.ds(8 * h, 1), :]
        mean = one * jnp.sum(total, axis=0, keepdims=True)
        row[g, pl.ds(8 * h, 8), :] = jnp.broadcast_to(mean, (8, 2 * tok))
        low = [((us[jj] * one) * (cut(dp, jj, tok) - mean)).astype(jnp.bfloat16) for jj in range(FAR - h)]
        accs[h] = dot(jnp.concatenate(low, 0), qs[g, h], NN)
        if h == 1:
            spread(core, accs, 0, (dkb,), g, tok)

    in_turn(groups, products, weigh, finish)


def near_grads(tok, groups, core_ref, lo_ref, qs, gs, kb, wk, ka, kc, vb, wv, va, vc, inv, row,
               dva, dvc, dka, dkc, dq0, dq1, dq_s):
    core = core_ref[0]
    lo_all = lo_ref[...]
    count = seen(lo_all, ka, tok) + seen(lo_all, kb, tok) + seen(lo_all, wk, tok)
    los = [first_keys(core, lo_all, count, h, tok) for h in range(2)]
    blocks = WINDOW // tok + 1

    def step(g, _):
        dvs, dks = [], []
        for h in range(2):
            k_rows = keys_of(core, ((kb, wk), ka, kc), range(h, h + blocks), g, tok)
            v_rows = keys_of(core, ((vb, wv), va, vc), range(h, h + blocks), g, tok)
            s = dot(k_rows, qs[g, h], NT)
            dp = dot(v_rows, gs[g, h], NT)
            one = inv[g, pl.ds(8 * h, 1), :]
            mean = row[g, pl.ds(8 * h, 1), :]
            low, dlow = [], []
            for jj in range(blocks):
                t, w = weights_of(cut(s, jj, tok), los[h], jj, jj == blocks - 1, tok)
                p = w * one
                low.append(p.astype(jnp.bfloat16))
                ds = p * slope(t) * (cut(dp, jj, tok) - mean)
                dlow.append(ds.astype(jnp.bfloat16))
            dvs.append(dot(jnp.concatenate(low[FAR - h :], 0), gs[g, h], NN))
            dks.append(dot(jnp.concatenate(dlow[FAR - h :], 0), qs[g, h], NN))
            dq_t = dot(k_rows.T, jnp.concatenate(dlow, 0), NN)
            dq_s[g, lax.bitwise_xor(core, h)] = dq_t.T.astype(jnp.bfloat16)
        spread(core, dvs, FAR, (dva, dvc), g, tok)
        spread(core, dks, FAR, (dka, dkc), g, tok)
        for r, dq in enumerate((dq0, dq1)):
            for hd in range(2):
                dq[:, lanes_at(2 * g + hd)] = dq_s[g, r, hd * tok : (hd + 1) * tok, :]
        return 0

    lax.fori_loop(0, groups, step, 0, unroll=True)


def merge(tok, groups, core_ref, mine, came, out):
    out[...] = (mine[...] + came[...].astype(jnp.float32)).astype(out.dtype)


def call(body, tok, groups, args, outs, scratch=()):
    vmem = pl.BlockSpec(memory_space=pltpu.VMEM)
    return pl.pallas_call(
        functools.partial(body, tok, groups),
        in_specs=[pl.BlockSpec(memory_space=pltpu.SMEM)] + [vmem] * (len(args) - 1),
        out_specs=[vmem] * len(outs),
        out_shape=[jax.ShapeDtypeStruct(s, d) for s, d in outs],
        scratch_shapes=list(scratch),
        compiler_params=pltpu.CompilerParams(vmem_limit_bytes=VMEM_LIMIT),
        name=body.__name__,
    )(*args)


VMEM_LIMIT = 16 * 1024 * 1024


def local(queries, keys, values, grad_out, segment):
    tok = queries.shape[0]
    kv_width = keys.shape[1]
    half = kv_width // 2
    groups = half // HEAD_DIM
    q_half = queries.shape[1] // 2
    bf16, f32 = jnp.bfloat16, jnp.float32
    core = lax.rem(lax.axis_index(AXES), 2)
    core_arr = core.reshape(1).astype(jnp.int32)

    def part(x, which, width):
        return lax.dynamic_slice(x, (0, which * width), (x.shape[0], width))

    k_in = swap(keys)
    seg_in = swap(segment)
    ids = jnp.concatenate([segment, seg_in]) + 1
    seg_rows = jnp.pad(ids.astype(bf16)[None, :], ((0, SEG_ROWS - 1), (0, half - 2 * tok)))
    kc = jnp.concatenate([part(keys, core, half), part(k_in, core, half), seg_rows], 0)
    v_in = swap(values)
    vc = jnp.concatenate([part(values, core, half), part(v_in, core, half), jnp.zeros((SEG_ROWS, half), bf16)], 0)
    ka = hop(kc, 1)
    va = hop(vc, 1)
    queries, grad_out, _ = lax.optimization_barrier((queries, grad_out, kc))
    qg_in = swap(jnp.concatenate([part(queries, 1 - core, q_half), part(grad_out, 1 - core, q_half)], 0))

    rows = ((groups, 2, 2 * tok, HEAD_DIM), bf16)
    stat = ((groups, 16, 2 * tok), f32)
    kv_f = ((2 * tok, half), f32)
    kv_b = ((2 * tok, half), bf16)
    dq_o = ((tok, q_half), bf16)

    qs, gs, lo = call(
        stack_heads, tok, groups, (core_arr, queries, grad_out, qg_in, kc),
        [rows, rows, ((8, tok), jnp.int32)])
    va, qs, gs, lo = lax.optimization_barrier((va, qs, gs, lo))
    wk = ahead(kc)
    wv = ahead(vc)
    kb = forward(ka)
    vb = forward(va)
    tot, term = call(
        near_sums, tok, groups, (core_arr, lo, qs, gs, ka, kc, va, vc), [stat, stat])
    dvb, inv = call(
        far_values, tok, groups, (core_arr, lo, qs, gs, ka, kb, wk, tot), [kv_b, stat])
    cv = hop(dvb, -1)
    dkb, row = call(
        far_keys, tok, groups, (core_arr, lo, qs, gs, ka, kb, wk, va, vb, wv, inv, term), [kv_b, stat])
    ck = hop(dkb, -1)
    dva, dvc, dka, dkc, dq0, dq1 = call(
        near_grads, tok, groups, (core_arr, lo, qs, gs, kb, wk, ka, kc, vb, wv, va, vc, inv, row),
        [kv_f, kv_f, kv_f, kv_f, dq_o, dq_o],
        [pltpu.VMEM((groups, 2, 2 * tok, HEAD_DIM), bf16)])
    (dv_out,) = call(merge, tok, groups, (core_arr, dva, cv), [kv_b])
    dv = hop(dv_out, -1)
    (dk_out,) = call(merge, tok, groups, (core_arr, dka, ck), [kv_b])
    dkc, dq1, _ = lax.optimization_barrier((dkc, dq1, dv_out))
    dk_same = hop(dk_out[:tok], -1)
    dk_cross = cross(dk_out[tok:], -1)
    def place(mine, other):
        first = jnp.where(core == 0, mine, other)
        second = jnp.where(core == 0, other, mine)
        return jnp.concatenate([first, second], 1)

    grad_q = place(dq0, swap(dq1))
    sum_v = dvc + dv.astype(f32)
    grad_v = place(sum_v[:tok].astype(bf16), swap(sum_v[tok:].astype(bf16)))
    other_k = swap(dkc[tok:])
    dk_cross, grad_v = lax.optimization_barrier((dk_cross, grad_v))
    same = (dkc[:tok] + dk_same.astype(f32)).astype(bf16)
    other = (other_k + dk_cross.astype(f32)).astype(bf16)
    grad_k = place(same, other)
    return grad_q, grad_k, grad_v


def solution(mesh):
    rows = P(AXES, None)
    return jax.shard_map(
        local,
        mesh=mesh,
        in_specs=(rows, rows, rows, rows, P(AXES)),
        out_specs=(rows, rows, rows),
        check_vma=False,
    )
```

```python
import functools

import jax
import jax.numpy as jnp
from jax import lax
from jax.experimental import pallas as pl
from jax.experimental.pallas import tpu as pltpu
from jax.sharding import PartitionSpec as P

HEAD_DIM = 128
WINDOW = 512
SOFTCAP = 50.0
SCALE = 1.0 / 12.0
LOG2E = 1.4426950408889634
AXES = ("ctx", "fsdp")
NT = (((1,), (1,)), ((), ()))
NN = (((1,), (0,)), ((), ()))
SEG_ROWS = 8
FAR = 2


def dot(a, b, dims):
    return lax.dot_general(a, b, dims, preferred_element_type=jnp.float32)


def swap(x):
    n = lax.axis_size(AXES)
    return lax.ppermute(x, AXES, [(i, i ^ 1) for i in range(n)])


def hop(x, chips):
    n = lax.axis_size(AXES)
    by = 2 * chips
    return lax.ppermute(x, AXES, [(i, i + by) for i in range(n) if 0 <= i + by < n])


def cross(x, chips):
    n = lax.axis_size(AXES)
    by = 2 * chips
    return lax.ppermute(x, AXES, [(i, (i ^ 1) + by) for i in range(n) if 0 <= i + by < n])


def forward(x):
    n, row = lax.axis_size(AXES), lax.axis_size("fsdp")
    return lax.ppermute(x, AXES, [(i, i + 2) for i in range(n) if i % row < row - 2])


def ahead(x):
    n, row = lax.axis_size(AXES), lax.axis_size("fsdp")
    return lax.ppermute(x, AXES, [(i, i + 4) for i in range(n - 4) if row - 4 <= i % row < row - 2])


def rows_at(core, half, tok):
    return pl.ds(pl.multiple_of(lax.bitwise_xor(core, half) * tok, tok), tok)


def lanes_at(g):
    return pl.ds(pl.multiple_of(g * HEAD_DIM, HEAD_DIM), HEAD_DIM)


def block_of(core, pieces, b, g, tok):
    parts = pieces[b // 2]
    at = (rows_at(core, b % 2, tok), lanes_at(g))
    return parts[0][at] + parts[1][at] if isinstance(parts, tuple) else parts[at]


def seen(lo, seg_ref, tok):
    ids = seg_ref[2 * tok : 2 * tok + 1, : 2 * tok].astype(jnp.float32)
    same = jnp.where(ids == lo[2:3, 0:1].astype(jnp.float32), 1.0, 0.0)
    return jnp.sum(same, axis=1, keepdims=True).astype(jnp.int32)


def first_keys(core, lo, count, half, tok):
    mine = jnp.where(core == half, lo[0:1], lo[1:2])
    mine = jnp.where(mine < 0, WINDOW - count, mine) - half * tok
    row = lax.broadcasted_iota(jnp.int32, (1, tok), 1)
    mine = jnp.maximum(mine, row + 1)
    return jnp.concatenate([mine, mine], 1)


def keys_of(core, pieces, blocks, g, tok):
    return jnp.concatenate([block_of(core, pieces, b, g, tok) for b in blocks], 0)


def weights_of(s, lo, jj, last, tok):
    t = jnp.tanh(s * (SCALE / SOFTCAP))
    w = jnp.exp2(t * (SOFTCAP * LOG2E))
    pos = lax.broadcasted_iota(jnp.int32, s.shape, 0)
    ok = pos >= lo - jj * tok
    if last:
        col = lax.broadcasted_iota(jnp.int32, s.shape, 1)
        ok = ok & (pos <= jnp.where(col >= tok, col - tok, col))
    return t, jnp.where(ok, w, 0.0)


def slope(t):
    return SCALE - t * t * SCALE


def cut(x, i, tok):
    return x[i * tok : (i + 1) * tok]


def fold(x):
    return jnp.sum(x.reshape(x.shape[0] // 8, 8, x.shape[1]), axis=0)


def stack_heads(tok, groups, core_ref, q, go, qgx, kc, qs, gs, lo):
    core = core_ref[0]
    ids = kc[2 * tok : 2 * tok + 1, : 2 * tok].astype(jnp.float32)
    column = jnp.broadcast_to(ids, (8, 2 * tok)).T[:, 0:1]
    before = jnp.sum(jnp.where(column < ids, 1.0, 0.0), axis=0, keepdims=True)
    first = jnp.min(ids, axis=1, keepdims=True)
    starts = jnp.where(ids == first, -1.0, WINDOW + before).astype(jnp.int32)
    lo[0:1, :] = starts[:, :tok]
    lo[1:2, :] = starts[:, tok:]
    lo[2:8, :] = jnp.broadcast_to(first.astype(jnp.int32), (6, tok))
    for g in range(groups):
        for hd in range(2):
            at = (core * groups + g) * 2 + hd
            here = pl.ds(hd * tok, tok)
            qs[g, core, here, :] = q[:, lanes_at(at)]
            gs[g, core, here, :] = go[:, lanes_at(at)]
            qs[g, 1 - core, here, :] = qgx[:tok, lanes_at(g * 2 + hd)]
            gs[g, 1 - core, here, :] = qgx[tok:, lanes_at(g * 2 + hd)]


def near_sums(tok, groups, core_ref, lo_ref, qs, gs, ka, kc, va, vc, tot, term):
    core = core_ref[0]
    lo_all = lo_ref[...]
    count = seen(lo_all, ka, tok)
    los = [first_keys(core, lo_all, count, h, tok) for h in range(2)]
    blocks = WINDOW // tok + 1

    def step(g, _):
        for h in range(2):
            near = range(h + FAR, h + blocks)
            s = dot(keys_of(core, (None, ka, kc), near, g, tok), qs[g, h], NT)
            dp = dot(keys_of(core, (None, va, vc), near, g, tok), gs[g, h], NT)
            total = jnp.zeros((8, 2 * tok), jnp.float32)
            mean = jnp.zeros((8, 2 * tok), jnp.float32)
            for jj in range(FAR, blocks):
                _, w = weights_of(cut(s, jj - FAR, tok), los[h], jj, jj == blocks - 1, tok)
                total = total + fold(w)
                mean = mean + fold(w * cut(dp, jj - FAR, tok))
            tot[g, pl.ds(8 * h, 8), :] = total
            term[g, pl.ds(8 * h, 8), :] = mean
        return 0

    lax.fori_loop(0, groups, step, 0, unroll=True)


def in_turn(groups, products, weigh, finish):
    units = [(g, h) for g in range(groups) for h in range(2)]
    ready, waiting = products(*units[0]), None
    for i, (g, h) in enumerate(units):
        ahead_of = products(*units[i + 1]) if i + 1 < len(units) else None
        held = weigh(g, h, ready)
        if waiting is not None:
            finish(*waiting)
        ready, waiting = ahead_of, (g, h, held)
    finish(*waiting)


def far_values(tok, groups, core_ref, lo_ref, qs, gs, ka, kb, wk, tot, dvb, inv):
    core = core_ref[0]
    lo_all = lo_ref[...]
    count = seen(lo_all, ka, tok) + seen(lo_all, kb, tok) + seen(lo_all, wk, tok)
    los = [first_keys(core, lo_all, count, h, tok) for h in range(2)]
    accs = {}

    def products(g, h):
        return dot(keys_of(core, ((kb, wk), ka), range(h, h + FAR), g, tok), qs[g, h], NT)

    def weigh(g, h, s):
        total = tot[g, pl.ds(8 * h, 8), :]
        ws = []
        for jj in range(FAR):
            _, w = weights_of(cut(s, jj, tok), los[h], jj, False, tok)
            total = total + fold(w)
            ws.append(w)
        return total, ws

    def finish(g, h, held):
        total, ws = held
        one = 1.0 / jnp.sum(total, axis=0, keepdims=True)
        inv[g, pl.ds(8 * h, 8), :] = jnp.broadcast_to(one, (8, 2 * tok))
        low = jnp.concatenate([(w * one).astype(jnp.bfloat16) for w in ws[: FAR - h]], 0)
        accs[h] = dot(low, gs[g, h], NN)
        if h == 1:
            spread(core, accs, 0, (dvb,), g, tok)

    in_turn(groups, products, weigh, finish)


def spread(core, accs, start, outs, g, tok):
    first = (start, max(start, 1))
    for b in range(start, start + 2 * len(outs)):
        acc = None
        for h in range(2):
            i = b - first[h]
            if 0 <= i < accs[h].shape[0] // tok:
                piece = cut(accs[h], i, tok)
                acc = piece if acc is None else acc + piece
        out = outs[(b - start) // 2]
        out[rows_at(core, b % 2, tok), lanes_at(g)] = acc.astype(out.dtype)


def far_keys(tok, groups, core_ref, lo_ref, qs, gs, ka, kb, wk, va, vb, wv, inv, term, dkb, row):
    core = core_ref[0]
    lo_all = lo_ref[...]
    count = seen(lo_all, ka, tok) + seen(lo_all, kb, tok) + seen(lo_all, wk, tok)
    los = [first_keys(core, lo_all, count, h, tok) for h in range(2)]
    accs = {}

    def products(g, h):
        blocks = range(h, h + FAR)
        return (
            dot(keys_of(core, ((kb, wk), ka), blocks, g, tok), qs[g, h], NT),
            dot(keys_of(core, ((vb, wv), va), blocks, g, tok), gs[g, h], NT),
        )

    def weigh(g, h, ready):
        s, dp = ready
        total = term[g, pl.ds(8 * h, 8), :]
        us = []
        for jj in range(FAR):
            t, w = weights_of(cut(s, jj, tok), los[h], jj, False, tok)
            total = total + fold(w * cut(dp, jj, tok))
            us.append(w * slope(t))
        return total, us, dp

    def finish(g, h, held):
        total, us, dp = held
        one = inv[g, pl.ds(8 * h, 1), :]
        mean = one * jnp.sum(total, axis=0, keepdims=True)
        row[g, pl.ds(8 * h, 8), :] = jnp.broadcast_to(mean, (8, 2 * tok))
        low = [((us[jj] * one) * (cut(dp, jj, tok) - mean)).astype(jnp.bfloat16) for jj in range(FAR - h)]
        accs[h] = dot(jnp.concatenate(low, 0), qs[g, h], NN)
        if h == 1:
            spread(core, accs, 0, (dkb,), g, tok)

    in_turn(groups, products, weigh, finish)


def near_grads(tok, groups, core_ref, lo_ref, qs, gs, kb, wk, ka, kc, vb, wv, va, vc, inv, row,
               dva, dvc, dka, dkc, dq0, dq1, dq_s):
    core = core_ref[0]
    lo_all = lo_ref[...]
    count = seen(lo_all, ka, tok) + seen(lo_all, kb, tok) + seen(lo_all, wk, tok)
    los = [first_keys(core, lo_all, count, h, tok) for h in range(2)]
    blocks = WINDOW // tok + 1

    def step(g, _):
        dvs, dks = [], []
        for h in range(2):
            k_rows = keys_of(core, ((kb, wk), ka, kc), range(h, h + blocks), g, tok)
            v_rows = keys_of(core, ((vb, wv), va, vc), range(h, h + blocks), g, tok)
            s = dot(k_rows, qs[g, h], NT)
            dp = dot(v_rows, gs[g, h], NT)
            one = inv[g, pl.ds(8 * h, 1), :]
            mean = row[g, pl.ds(8 * h, 1), :]
            low, dlow = [], []
            for jj in range(blocks):
                t, w = weights_of(cut(s, jj, tok), los[h], jj, jj == blocks - 1, tok)
                p = w * one
                low.append(p.astype(jnp.bfloat16))
                ds = p * slope(t) * (cut(dp, jj, tok) - mean)
                dlow.append(ds.astype(jnp.bfloat16))
            dvs.append(dot(jnp.concatenate(low[FAR - h :], 0), gs[g, h], NN))
            dks.append(dot(jnp.concatenate(dlow[FAR - h :], 0), qs[g, h], NN))
            dq_t = dot(k_rows.T, jnp.concatenate(dlow, 0), NN)
            dq_s[g, lax.bitwise_xor(core, h)] = dq_t.T.astype(jnp.bfloat16)
        spread(core, dvs, FAR, (dva, dvc), g, tok)
        spread(core, dks, FAR, (dka, dkc), g, tok)
        for r, dq in enumerate((dq0, dq1)):
            for hd in range(2):
                dq[:, lanes_at(2 * g + hd)] = dq_s[g, r, hd * tok : (hd + 1) * tok, :]
        return 0

    lax.fori_loop(0, groups, step, 0, unroll=True)


def merge(tok, groups, core_ref, mine, came, out):
    out[...] = (mine[...] + came[...].astype(jnp.float32)).astype(out.dtype)


def call(body, tok, groups, args, outs, scratch=()):
    vmem = pl.BlockSpec(memory_space=pltpu.VMEM)
    return pl.pallas_call(
        functools.partial(body, tok, groups),
        in_specs=[pl.BlockSpec(memory_space=pltpu.SMEM)] + [vmem] * (len(args) - 1),
        out_specs=[vmem] * len(outs),
        out_shape=[jax.ShapeDtypeStruct(s, d) for s, d in outs],
        scratch_shapes=list(scratch),
        compiler_params=pltpu.CompilerParams(vmem_limit_bytes=VMEM_LIMIT),
        name=body.__name__,
    )(*args)


VMEM_LIMIT = 16 * 1024 * 1024


def local(queries, keys, values, grad_out, segment):
    tok = queries.shape[0]
    kv_width = keys.shape[1]
    half = kv_width // 2
    groups = half // HEAD_DIM
    q_half = queries.shape[1] // 2
    bf16, f32 = jnp.bfloat16, jnp.float32
    core = lax.rem(lax.axis_index(AXES), 2)
    core_arr = core.reshape(1).astype(jnp.int32)

    def part(x, which, width):
        return lax.dynamic_slice(x, (0, which * width), (x.shape[0], width))

    k_in = swap(keys)
    seg_in = swap(segment)
    ids = jnp.concatenate([segment, seg_in]) + 1
    seg_rows = jnp.pad(ids.astype(bf16)[None, :], ((0, SEG_ROWS - 1), (0, half - 2 * tok)))
    kc = jnp.concatenate([part(keys, core, half), part(k_in, core, half), seg_rows], 0)
    v_in = swap(values)
    values, _ = lax.optimization_barrier((values, kc))
    vc = jnp.concatenate([part(values, core, half), part(v_in, core, half)], 0)
    ka = hop(kc, 1)
    va = hop(vc, 1)
    queries, grad_out, _ = lax.optimization_barrier((queries, grad_out, kc))
    qg_in = swap(jnp.concatenate([part(queries, 1 - core, q_half), part(grad_out, 1 - core, q_half)], 0))

    rows = ((groups, 2, 2 * tok, HEAD_DIM), bf16)
    stat = ((groups, 16, 2 * tok), f32)
    kv_f = ((2 * tok, half), f32)
    kv_b = ((2 * tok, half), bf16)
    dq_o = ((tok, q_half), bf16)

    qs, gs, lo = call(
        stack_heads, tok, groups, (core_arr, queries, grad_out, qg_in, kc),
        [rows, rows, ((8, tok), jnp.int32)])
    va, qs, gs, lo = lax.optimization_barrier((va, qs, gs, lo))
    wk = ahead(kc)
    wv = ahead(vc)
    kb = forward(ka)
    vb = forward(va)
    tot, term = call(
        near_sums, tok, groups, (core_arr, lo, qs, gs, ka, kc, va, vc), [stat, stat])
    dvb, inv = call(
        far_values, tok, groups, (core_arr, lo, qs, gs, ka, kb, wk, tot), [kv_b, stat])
    cv = hop(dvb, -1)
    dkb, row = call(
        far_keys, tok, groups, (core_arr, lo, qs, gs, ka, kb, wk, va, vb, wv, inv, term), [kv_b, stat])
    ck = hop(dkb, -1)
    dva, dvc, dka, dkc, dq0, dq1 = call(
        near_grads, tok, groups, (core_arr, lo, qs, gs, kb, wk, ka, kc, vb, wv, va, vc, inv, row),
        [kv_f, kv_f, kv_f, kv_f, dq_o, dq_o],
        [pltpu.VMEM((groups, 2, 2 * tok, HEAD_DIM), bf16)])
    (dv_out,) = call(merge, tok, groups, (core_arr, dva, cv), [kv_b])
    dv = hop(dv_out, -1)
    (dk_out,) = call(merge, tok, groups, (core_arr, dka, ck), [kv_b])
    dkc, dq1, _ = lax.optimization_barrier((dkc, dq1, dv_out))
    dk_same = hop(dk_out[:tok], -1)
    dk_cross = cross(dk_out[tok:], -1)
    def place(mine, other):
        first = jnp.where(core == 0, mine, other)
        second = jnp.where(core == 0, other, mine)
        return jnp.concatenate([first, second], 1)

    grad_q = place(dq0, swap(dq1))
    sum_v = dvc + dv.astype(f32)
    grad_v = place(sum_v[:tok].astype(bf16), swap(sum_v[tok:].astype(bf16)))
    other_k = swap(dkc[tok:])
    dk_cross, grad_v = lax.optimization_barrier((dk_cross, grad_v))
    same = (dkc[:tok] + dk_same.astype(f32)).astype(bf16)
    other = (other_k + dk_cross.astype(f32)).astype(bf16)
    grad_k = place(same, other)
    return grad_q, grad_k, grad_v


def solution(mesh):
    rows = P(AXES, None)
    return jax.shard_map(
        local,
        mesh=mesh,
        in_specs=(rows, rows, rows, rows, P(AXES)),
        out_specs=(rows, rows, rows),
        check_vma=False,
    )
```

```python
import functools

import jax
import jax.numpy as jnp
from jax import lax
from jax.experimental import pallas as pl
from jax.experimental.pallas import tpu as pltpu
from jax.sharding import PartitionSpec as P

HEAD_DIM = 128
WINDOW = 512
SOFTCAP = 50.0
SCALE = 1.0 / 12.0
LOG2E = 1.4426950408889634
AXES = ("ctx", "fsdp")
NT = (((1,), (1,)), ((), ()))
NN = (((1,), (0,)), ((), ()))
SEG_ROWS = 8
FAR = 2


def dot(a, b, dims):
    return lax.dot_general(a, b, dims, preferred_element_type=jnp.float32)


def swap(x):
    n = lax.axis_size(AXES)
    return lax.ppermute(x, AXES, [(i, i ^ 1) for i in range(n)])


def hop(x, chips):
    n = lax.axis_size(AXES)
    by = 2 * chips
    return lax.ppermute(x, AXES, [(i, i + by) for i in range(n) if 0 <= i + by < n])


def cross(x, chips):
    n = lax.axis_size(AXES)
    by = 2 * chips
    return lax.ppermute(x, AXES, [(i, (i ^ 1) + by) for i in range(n) if 0 <= i + by < n])


def forward(x):
    n, row = lax.axis_size(AXES), lax.axis_size("fsdp")
    return lax.ppermute(x, AXES, [(i, i + 2) for i in range(n) if i % row < row - 2])


def ahead(x):
    n, row = lax.axis_size(AXES), lax.axis_size("fsdp")
    return lax.ppermute(x, AXES, [(i, i + 4) for i in range(n - 4) if row - 4 <= i % row < row - 2])


def rows_at(core, half, tok):
    return pl.ds(pl.multiple_of(lax.bitwise_xor(core, half) * tok, tok), tok)


def lanes_at(g):
    return pl.ds(pl.multiple_of(g * HEAD_DIM, HEAD_DIM), HEAD_DIM)


def block_of(core, pieces, b, g, tok):
    parts = pieces[b // 2]
    at = (rows_at(core, b % 2, tok), lanes_at(g))
    return parts[0][at] + parts[1][at] if isinstance(parts, tuple) else parts[at]


def seen(lo, seg_ref, tok):
    ids = seg_ref[2 * tok : 2 * tok + 1, : 2 * tok].astype(jnp.float32)
    same = jnp.where(ids == lo[2:3, 0:1].astype(jnp.float32), 1.0, 0.0)
    return jnp.sum(same, axis=1, keepdims=True).astype(jnp.int32)


def first_keys(core, lo, count, half, tok):
    mine = jnp.where(core == half, lo[0:1], lo[1:2])
    mine = jnp.where(mine < 0, WINDOW - count, mine) - half * tok
    row = lax.broadcasted_iota(jnp.int32, (1, tok), 1)
    mine = jnp.maximum(mine, row + 1)
    return jnp.concatenate([mine, mine], 1)


def keys_of(core, pieces, blocks, g, tok):
    return jnp.concatenate([block_of(core, pieces, b, g, tok) for b in blocks], 0)


def weights_of(s, lo, jj, last, tok):
    t = jnp.tanh(s * (SCALE / SOFTCAP))
    w = jnp.exp2(t * (SOFTCAP * LOG2E))
    pos = lax.broadcasted_iota(jnp.int32, s.shape, 0)
    ok = pos >= lo - jj * tok
    if last:
        col = lax.broadcasted_iota(jnp.int32, s.shape, 1)
        ok = ok & (pos <= jnp.where(col >= tok, col - tok, col))
    return t, jnp.where(ok, w, 0.0)


def slope(t):
    return SCALE - t * t * SCALE


def cut(x, i, tok):
    return x[i * tok : (i + 1) * tok]


def fold(x):
    return jnp.sum(x.reshape(x.shape[0] // 8, 8, x.shape[1]), axis=0)


def stack_heads(tok, groups, core_ref, q, go, qgx, kc, qs, gs, lo):
    core = core_ref[0]
    ids = kc[2 * tok : 2 * tok + 1, : 2 * tok].astype(jnp.float32)
    column = jnp.broadcast_to(ids, (8, 2 * tok)).T[:, 0:1]
    before = jnp.sum(jnp.where(column < ids, 1.0, 0.0), axis=0, keepdims=True)
    first = jnp.min(ids, axis=1, keepdims=True)
    starts = jnp.where(ids == first, -1.0, WINDOW + before).astype(jnp.int32)
    lo[0:1, :] = starts[:, :tok]
    lo[1:2, :] = starts[:, tok:]
    lo[2:8, :] = jnp.broadcast_to(first.astype(jnp.int32), (6, tok))
    for g in range(groups):
        for hd in range(2):
            at = (core * groups + g) * 2 + hd
            here = pl.ds(hd * tok, tok)
            qs[g, core, here, :] = q[:, lanes_at(at)]
            gs[g, core, here, :] = go[:, lanes_at(at)]
            qs[g, 1 - core, here, :] = qgx[:tok, lanes_at(g * 2 + hd)]
            gs[g, 1 - core, here, :] = qgx[tok:, lanes_at(g * 2 + hd)]


def near_sums(tok, groups, core_ref, lo_ref, qs, gs, ka, kc, va, vc, tot, term):
    core = core_ref[0]
    lo_all = lo_ref[...]
    count = seen(lo_all, ka, tok)
    los = [first_keys(core, lo_all, count, h, tok) for h in range(2)]
    blocks = WINDOW // tok + 1

    def products(g, h):
        near = range(h + FAR, h + blocks)
        return (
            dot(keys_of(core, (None, ka, kc), near, g, tok), qs[g, h], NT),
            dot(keys_of(core, (None, va, vc), near, g, tok), gs[g, h], NT),
        )

    def weigh(g, h, ready):
        s, dp = ready
        total = jnp.zeros((8, 2 * tok), jnp.float32)
        mean = jnp.zeros((8, 2 * tok), jnp.float32)
        for jj in range(FAR, blocks):
            _, w = weights_of(cut(s, jj - FAR, tok), los[h], jj, jj == blocks - 1, tok)
            total = total + fold(w)
            mean = mean + fold(w * cut(dp, jj - FAR, tok))
        return total, mean

    def finish(g, h, held):
        tot[g, pl.ds(8 * h, 8), :] = held[0]
        term[g, pl.ds(8 * h, 8), :] = held[1]

    in_turn(groups, products, weigh, finish)


def in_turn(groups, products, weigh, finish):
    units = [(g, h) for g in range(groups) for h in range(2)]
    ready, waiting = products(*units[0]), None
    for i, (g, h) in enumerate(units):
        ahead_of = products(*units[i + 1]) if i + 1 < len(units) else None
        held = weigh(g, h, ready)
        if waiting is not None:
            finish(*waiting)
        ready, waiting = ahead_of, (g, h, held)
    finish(*waiting)


def far_values(tok, groups, core_ref, lo_ref, qs, gs, ka, kb, wk, tot, dvb, inv):
    core = core_ref[0]
    lo_all = lo_ref[...]
    count = seen(lo_all, ka, tok) + seen(lo_all, kb, tok) + seen(lo_all, wk, tok)
    los = [first_keys(core, lo_all, count, h, tok) for h in range(2)]
    accs = {}

    def products(g, h):
        return dot(keys_of(core, ((kb, wk), ka), range(h, h + FAR), g, tok), qs[g, h], NT)

    def weigh(g, h, s):
        total = tot[g, pl.ds(8 * h, 8), :]
        ws = []
        for jj in range(FAR):
            _, w = weights_of(cut(s, jj, tok), los[h], jj, False, tok)
            total = total + fold(w)
            ws.append(w)
        return total, ws

    def finish(g, h, held):
        total, ws = held
        one = 1.0 / jnp.sum(total, axis=0, keepdims=True)
        inv[g, pl.ds(8 * h, 8), :] = jnp.broadcast_to(one, (8, 2 * tok))
        low = jnp.concatenate([(w * one).astype(jnp.bfloat16) for w in ws[: FAR - h]], 0)
        accs[h] = dot(low, gs[g, h], NN)
        if h == 1:
            spread(core, accs, 0, (dvb,), g, tok)

    in_turn(groups, products, weigh, finish)


def spread(core, accs, start, outs, g, tok):
    first = (start, max(start, 1))
    for b in range(start, start + 2 * len(outs)):
        acc = None
        for h in range(2):
            i = b - first[h]
            if 0 <= i < accs[h].shape[0] // tok:
                piece = cut(accs[h], i, tok)
                acc = piece if acc is None else acc + piece
        out = outs[(b - start) // 2]
        out[rows_at(core, b % 2, tok), lanes_at(g)] = acc.astype(out.dtype)


def far_keys(tok, groups, core_ref, lo_ref, qs, gs, ka, kb, wk, va, vb, wv, inv, term, dkb, row):
    core = core_ref[0]
    lo_all = lo_ref[...]
    count = seen(lo_all, ka, tok) + seen(lo_all, kb, tok) + seen(lo_all, wk, tok)
    los = [first_keys(core, lo_all, count, h, tok) for h in range(2)]
    accs = {}

    def products(g, h):
        blocks = range(h, h + FAR)
        return (
            dot(keys_of(core, ((kb, wk), ka), blocks, g, tok), qs[g, h], NT),
            dot(keys_of(core, ((vb, wv), va), blocks, g, tok), gs[g, h], NT),
        )

    def weigh(g, h, ready):
        s, dp = ready
        total = term[g, pl.ds(8 * h, 8), :]
        us = []
        for jj in range(FAR):
            t, w = weights_of(cut(s, jj, tok), los[h], jj, False, tok)
            total = total + fold(w * cut(dp, jj, tok))
            us.append(w * slope(t))
        return total, us, dp

    def finish(g, h, held):
        total, us, dp = held
        one = inv[g, pl.ds(8 * h, 1), :]
        mean = one * jnp.sum(total, axis=0, keepdims=True)
        row[g, pl.ds(8 * h, 8), :] = jnp.broadcast_to(mean, (8, 2 * tok))
        low = [((us[jj] * one) * (cut(dp, jj, tok) - mean)).astype(jnp.bfloat16) for jj in range(FAR - h)]
        accs[h] = dot(jnp.concatenate(low, 0), qs[g, h], NN)
        if h == 1:
            spread(core, accs, 0, (dkb,), g, tok)

    in_turn(groups, products, weigh, finish)


def near_grads(tok, groups, core_ref, lo_ref, qs, gs, kb, wk, ka, kc, vb, wv, va, vc, inv, row,
               dva, dvc, dka, dkc, dq0, dq1, dq_s):
    core = core_ref[0]
    lo_all = lo_ref[...]
    count = seen(lo_all, ka, tok) + seen(lo_all, kb, tok) + seen(lo_all, wk, tok)
    los = [first_keys(core, lo_all, count, h, tok) for h in range(2)]
    blocks = WINDOW // tok + 1

    def step(g, _):
        dvs, dks = [], []
        for h in range(2):
            k_rows = keys_of(core, ((kb, wk), ka, kc), range(h, h + blocks), g, tok)
            v_rows = keys_of(core, ((vb, wv), va, vc), range(h, h + blocks), g, tok)
            s = dot(k_rows, qs[g, h], NT)
            dp = dot(v_rows, gs[g, h], NT)
            one = inv[g, pl.ds(8 * h, 1), :]
            mean = row[g, pl.ds(8 * h, 1), :]
            low, dlow = [], []
            for jj in range(blocks):
                t, w = weights_of(cut(s, jj, tok), los[h], jj, jj == blocks - 1, tok)
                p = w * one
                low.append(p.astype(jnp.bfloat16))
                ds = p * slope(t) * (cut(dp, jj, tok) - mean)
                dlow.append(ds.astype(jnp.bfloat16))
            dvs.append(dot(jnp.concatenate(low[FAR - h :], 0), gs[g, h], NN))
            dks.append(dot(jnp.concatenate(dlow[FAR - h :], 0), qs[g, h], NN))
            dq_t = dot(k_rows.T, jnp.concatenate(dlow, 0), NN)
            dq_s[g, lax.bitwise_xor(core, h)] = dq_t.T.astype(jnp.bfloat16)
        spread(core, dvs, FAR, (dva, dvc), g, tok)
        spread(core, dks, FAR, (dka, dkc), g, tok)
        for r, dq in enumerate((dq0, dq1)):
            for hd in range(2):
                dq[:, lanes_at(2 * g + hd)] = dq_s[g, r, hd * tok : (hd + 1) * tok, :]
        return 0

    lax.fori_loop(0, groups, step, 0, unroll=True)


def merge(tok, groups, core_ref, mine, came, out):
    out[...] = (mine[...] + came[...].astype(jnp.float32)).astype(out.dtype)


def call(body, tok, groups, args, outs, scratch=()):
    vmem = pl.BlockSpec(memory_space=pltpu.VMEM)
    return pl.pallas_call(
        functools.partial(body, tok, groups),
        in_specs=[pl.BlockSpec(memory_space=pltpu.SMEM)] + [vmem] * (len(args) - 1),
        out_specs=[vmem] * len(outs),
        out_shape=[jax.ShapeDtypeStruct(s, d) for s, d in outs],
        scratch_shapes=list(scratch),
        compiler_params=pltpu.CompilerParams(vmem_limit_bytes=VMEM_LIMIT),
        name=body.__name__,
    )(*args)


VMEM_LIMIT = 16 * 1024 * 1024


def local(queries, keys, values, grad_out, segment):
    tok = queries.shape[0]
    kv_width = keys.shape[1]
    half = kv_width // 2
    groups = half // HEAD_DIM
    q_half = queries.shape[1] // 2
    bf16, f32 = jnp.bfloat16, jnp.float32
    core = lax.rem(lax.axis_index(AXES), 2)
    core_arr = core.reshape(1).astype(jnp.int32)

    def part(x, which, width):
        return lax.dynamic_slice(x, (0, which * width), (x.shape[0], width))

    k_in = swap(keys)
    seg_in = swap(segment)
    ids = jnp.concatenate([segment, seg_in]) + 1
    seg_rows = jnp.pad(ids.astype(bf16)[None, :], ((0, SEG_ROWS - 1), (0, half - 2 * tok)))
    kc = jnp.concatenate([part(keys, core, half), part(k_in, core, half), seg_rows], 0)
    v_in = swap(values)
    values, _ = lax.optimization_barrier((values, kc))
    vc = jnp.concatenate([part(values, core, half), part(v_in, core, half)], 0)
    ka = hop(kc, 1)
    va = hop(vc, 1)
    queries, grad_out, _ = lax.optimization_barrier((queries, grad_out, kc))
    qg_in = swap(jnp.concatenate([part(queries, 1 - core, q_half), part(grad_out, 1 - core, q_half)], 0))

    rows = ((groups, 2, 2 * tok, HEAD_DIM), bf16)
    stat = ((groups, 16, 2 * tok), f32)
    kv_f = ((2 * tok, half), f32)
    kv_b = ((2 * tok, half), bf16)
    dq_o = ((tok, q_half), bf16)

    qs, gs, lo = call(
        stack_heads, tok, groups, (core_arr, queries, grad_out, qg_in, kc),
        [rows, rows, ((8, tok), jnp.int32)])
    va, qs, gs, lo = lax.optimization_barrier((va, qs, gs, lo))
    wk = ahead(kc)
    wv = ahead(vc)
    kb = forward(ka)
    vb = forward(va)
    tot, term = call(
        near_sums, tok, groups, (core_arr, lo, qs, gs, ka, kc, va, vc), [stat, stat])
    dvb, inv = call(
        far_values, tok, groups, (core_arr, lo, qs, gs, ka, kb, wk, tot), [kv_b, stat])
    cv = hop(dvb, -1)
    dkb, row = call(
        far_keys, tok, groups, (core_arr, lo, qs, gs, ka, kb, wk, va, vb, wv, inv, term), [kv_b, stat])
    ck = hop(dkb, -1)
    dva, dvc, dka, dkc, dq0, dq1 = call(
        near_grads, tok, groups, (core_arr, lo, qs, gs, kb, wk, ka, kc, vb, wv, va, vc, inv, row),
        [kv_f, kv_f, kv_f, kv_f, dq_o, dq_o],
        [pltpu.VMEM((groups, 2, 2 * tok, HEAD_DIM), bf16)])
    (dv_out,) = call(merge, tok, groups, (core_arr, dva, cv), [kv_b])
    dv = hop(dv_out, -1)
    (dk_out,) = call(merge, tok, groups, (core_arr, dka, ck), [kv_b])
    dkc, dq1, _ = lax.optimization_barrier((dkc, dq1, dv_out))
    dk_same = hop(dk_out[:tok], -1)
    dk_cross = cross(dk_out[tok:], -1)
    def place(mine, other):
        first = jnp.where(core == 0, mine, other)
        second = jnp.where(core == 0, other, mine)
        return jnp.concatenate([first, second], 1)

    grad_q = place(dq0, swap(dq1))
    sum_v = dvc + dv.astype(f32)
    grad_v = place(sum_v[:tok].astype(bf16), swap(sum_v[tok:].astype(bf16)))
    other_k = swap(dkc[tok:])
    dk_cross, grad_v = lax.optimization_barrier((dk_cross, grad_v))
    same = (dkc[:tok] + dk_same.astype(f32)).astype(bf16)
    other = (other_k + dk_cross.astype(f32)).astype(bf16)
    grad_k = place(same, other)
    return grad_q, grad_k, grad_v


def solution(mesh):
    rows = P(AXES, None)
    return jax.shard_map(
        local,
        mesh=mesh,
        in_specs=(rows, rows, rows, rows, P(AXES)),
        out_specs=(rows, rows, rows),
        check_vma=False,
    )
```

```python
import functools

import jax
import jax.numpy as jnp
from jax import lax
from jax.experimental import pallas as pl
from jax.experimental.pallas import tpu as pltpu
from jax.sharding import PartitionSpec as P

HEAD_DIM = 128
WINDOW = 512
SOFTCAP = 50.0
SCALE = 1.0 / 12.0
LOG2E = 1.4426950408889634
AXES = ("ctx", "fsdp")
NT = (((1,), (1,)), ((), ()))
NN = (((1,), (0,)), ((), ()))
SEG_ROWS = 8
FAR = 2


def dot(a, b, dims):
    return lax.dot_general(a, b, dims, preferred_element_type=jnp.float32)


def swap(x):
    n = lax.axis_size(AXES)
    return lax.ppermute(x, AXES, [(i, i ^ 1) for i in range(n)])


def hop(x, chips):
    n = lax.axis_size(AXES)
    by = 2 * chips
    return lax.ppermute(x, AXES, [(i, i + by) for i in range(n) if 0 <= i + by < n])


def cross(x, chips):
    n = lax.axis_size(AXES)
    by = 2 * chips
    return lax.ppermute(x, AXES, [(i, (i ^ 1) + by) for i in range(n) if 0 <= i + by < n])


def forward(x):
    n, row = lax.axis_size(AXES), lax.axis_size("fsdp")
    return lax.ppermute(x, AXES, [(i, i + 2) for i in range(n) if i % row < row - 2])


def ahead(x):
    n, row = lax.axis_size(AXES), lax.axis_size("fsdp")
    return lax.ppermute(x, AXES, [(i, i + 4) for i in range(n - 4) if row - 4 <= i % row < row - 2])


def rows_at(core, half, tok):
    return pl.ds(pl.multiple_of(lax.bitwise_xor(core, half) * tok, tok), tok)


def lanes_at(g):
    return pl.ds(pl.multiple_of(g * HEAD_DIM, HEAD_DIM), HEAD_DIM)


def block_of(core, pieces, b, g, tok):
    parts = pieces[b // 2]
    at = (rows_at(core, b % 2, tok), lanes_at(g))
    return parts[0][at] + parts[1][at] if isinstance(parts, tuple) else parts[at]


def seen(lo, seg_ref, tok):
    ids = seg_ref[2 * tok : 2 * tok + 1, : 2 * tok].astype(jnp.float32)
    same = jnp.where(ids == lo[2:3, 0:1].astype(jnp.float32), 1.0, 0.0)
    return jnp.sum(same, axis=1, keepdims=True).astype(jnp.int32)


def first_keys(core, lo, count, half, tok):
    mine = jnp.where(core == half, lo[0:1], lo[1:2])
    mine = jnp.where(mine < 0, WINDOW - count, mine) - half * tok
    row = lax.broadcasted_iota(jnp.int32, (1, tok), 1)
    mine = jnp.maximum(mine, row + 1)
    return jnp.concatenate([mine, mine], 1)


def keys_of(core, pieces, blocks, g, tok):
    return jnp.concatenate([block_of(core, pieces, b, g, tok) for b in blocks], 0)


def weights_of(s, lo, jj, last, tok):
    t = jnp.tanh(s * (SCALE / SOFTCAP))
    w = jnp.exp2(t * (SOFTCAP * LOG2E))
    pos = lax.broadcasted_iota(jnp.int32, s.shape, 0)
    ok = pos >= lo - jj * tok
    if last:
        col = lax.broadcasted_iota(jnp.int32, s.shape, 1)
        ok = ok & (pos <= jnp.where(col >= tok, col - tok, col))
    return t, jnp.where(ok, w, 0.0)


def slope(t):
    return SCALE - t * t * SCALE


def cut(x, i, tok):
    return x[i * tok : (i + 1) * tok]


def fold(x):
    return jnp.sum(x.reshape(x.shape[0] // 8, 8, x.shape[1]), axis=0)


def stack_heads(tok, groups, core_ref, q, go, qgx, kc, qs, gs, lo):
    core = core_ref[0]
    ids = kc[2 * tok : 2 * tok + 1, : 2 * tok].astype(jnp.float32)
    column = jnp.broadcast_to(ids, (8, 2 * tok)).T[:, 0:1]
    before = jnp.sum(jnp.where(column < ids, 1.0, 0.0), axis=0, keepdims=True)
    first = jnp.min(ids, axis=1, keepdims=True)
    starts = jnp.where(ids == first, -1.0, WINDOW + before).astype(jnp.int32)
    lo[0:1, :] = starts[:, :tok]
    lo[1:2, :] = starts[:, tok:]
    lo[2:8, :] = jnp.broadcast_to(first.astype(jnp.int32), (6, tok))
    for g in range(groups):
        for hd in range(2):
            at = (core * groups + g) * 2 + hd
            here = pl.ds(hd * tok, tok)
            qs[g, core, here, :] = q[:, lanes_at(at)]
            gs[g, core, here, :] = go[:, lanes_at(at)]
            qs[g, 1 - core, here, :] = qgx[:tok, lanes_at(g * 2 + hd)]
            gs[g, 1 - core, here, :] = qgx[tok:, lanes_at(g * 2 + hd)]


def near_sums(tok, groups, core_ref, lo_ref, qs, gs, ka, kc, va, vc, tot, term):
    core = core_ref[0]
    lo_all = lo_ref[...]
    count = seen(lo_all, ka, tok)
    los = [first_keys(core, lo_all, count, h, tok) for h in range(2)]
    blocks = WINDOW // tok + 1

    def products(g, h):
        near = range(h + FAR, h + blocks)
        return (
            dot(keys_of(core, (None, ka, kc), near, g, tok), qs[g, h], NT),
            dot(keys_of(core, (None, va, vc), near, g, tok), gs[g, h], NT),
        )

    def weigh(g, h, ready):
        s, dp = ready
        total = jnp.zeros((8, 2 * tok), jnp.float32)
        mean = jnp.zeros((8, 2 * tok), jnp.float32)
        for jj in range(FAR, blocks):
            _, w = weights_of(cut(s, jj - FAR, tok), los[h], jj, jj == blocks - 1, tok)
            total = total + fold(w)
            mean = mean + fold(w * cut(dp, jj - FAR, tok))
        return total, mean

    def finish(g, h, held):
        tot[g, pl.ds(8 * h, 8), :] = held[0]
        term[g, pl.ds(8 * h, 8), :] = held[1]

    in_turn(groups, products, weigh, finish)


def in_turn(groups, products, weigh, finish):
    units = [(g, h) for g in range(groups) for h in range(2)]
    ready, waiting = products(*units[0]), None
    for i, (g, h) in enumerate(units):
        ahead_of = products(*units[i + 1]) if i + 1 < len(units) else None
        held = weigh(g, h, ready)
        if waiting is not None:
            finish(*waiting)
        ready, waiting = ahead_of, (g, h, held)
    finish(*waiting)


def far_values(tok, groups, core_ref, lo_ref, qs, gs, ka, kb, wk, tot, dvb, inv):
    core = core_ref[0]
    lo_all = lo_ref[...]
    count = seen(lo_all, ka, tok) + seen(lo_all, kb, tok) + seen(lo_all, wk, tok)
    los = [first_keys(core, lo_all, count, h, tok) for h in range(2)]
    accs = {}

    def products(g, h):
        return dot(keys_of(core, ((kb, wk), ka), range(h, h + FAR), g, tok), qs[g, h], NT)

    def weigh(g, h, s):
        total = tot[g, pl.ds(8 * h, 8), :]
        ws = []
        for jj in range(FAR):
            _, w = weights_of(cut(s, jj, tok), los[h], jj, False, tok)
            total = total + fold(w)
            ws.append(w)
        return total, ws

    def finish(g, h, held):
        total, ws = held
        one = 1.0 / jnp.sum(total, axis=0, keepdims=True)
        inv[g, pl.ds(8 * h, 8), :] = jnp.broadcast_to(one, (8, 2 * tok))
        low = jnp.concatenate([(w * one).astype(jnp.bfloat16) for w in ws[: FAR - h]], 0)
        accs[h] = dot(low, gs[g, h], NN)
        if h == 1:
            spread(core, accs, 0, (dvb,), g, tok)

    in_turn(groups, products, weigh, finish)


def spread(core, accs, start, outs, g, tok):
    first = (start, max(start, 1))
    for b in range(start, start + 2 * len(outs)):
        acc = None
        for h in range(2):
            i = b - first[h]
            if 0 <= i < accs[h].shape[0] // tok:
                piece = cut(accs[h], i, tok)
                acc = piece if acc is None else acc + piece
        out = outs[(b - start) // 2]
        out[rows_at(core, b % 2, tok), lanes_at(g)] = acc.astype(out.dtype)


def far_keys(tok, groups, core_ref, lo_ref, qs, gs, ka, kb, wk, va, vb, wv, inv, term, dkb, row):
    core = core_ref[0]
    lo_all = lo_ref[...]
    count = seen(lo_all, ka, tok) + seen(lo_all, kb, tok) + seen(lo_all, wk, tok)
    los = [first_keys(core, lo_all, count, h, tok) for h in range(2)]
    accs = {}

    def products(g, h):
        blocks = range(h, h + FAR)
        return (
            dot(keys_of(core, ((kb, wk), ka), blocks, g, tok), qs[g, h], NT),
            dot(keys_of(core, ((vb, wv), va), blocks, g, tok), gs[g, h], NT),
        )

    def weigh(g, h, ready):
        s, dp = ready
        total = term[g, pl.ds(8 * h, 8), :]
        us = []
        for jj in range(FAR):
            t, w = weights_of(cut(s, jj, tok), los[h], jj, False, tok)
            total = total + fold(w * cut(dp, jj, tok))
            us.append(w * slope(t))
        return total, us, dp

    def finish(g, h, held):
        total, us, dp = held
        one = inv[g, pl.ds(8 * h, 1), :]
        mean = one * jnp.sum(total, axis=0, keepdims=True)
        row[g, pl.ds(8 * h, 8), :] = jnp.broadcast_to(mean, (8, 2 * tok))
        low = [((us[jj] * one) * (cut(dp, jj, tok) - mean)).astype(jnp.bfloat16) for jj in range(FAR - h)]
        accs[h] = dot(jnp.concatenate(low, 0), qs[g, h], NN)
        if h == 1:
            spread(core, accs, 0, (dkb,), g, tok)

    in_turn(groups, products, weigh, finish)


def near_grads(tok, groups, core_ref, lo_ref, qs, gs, kb, wk, ka, kc, vb, wv, va, vc, inv, row,
               dva, dvc, dka, dkc, dq0, dq1, dq_s):
    core = core_ref[0]
    lo_all = lo_ref[...]
    count = seen(lo_all, ka, tok) + seen(lo_all, kb, tok) + seen(lo_all, wk, tok)
    los = [first_keys(core, lo_all, count, h, tok) for h in range(2)]
    blocks = WINDOW // tok + 1

    def step(g, _):
        dvs, dks = [], []
        for h in range(2):
            k_rows = keys_of(core, ((kb, wk), ka, kc), range(h, h + blocks), g, tok)
            v_rows = keys_of(core, ((vb, wv), va, vc), range(h, h + blocks), g, tok)
            s = dot(k_rows, qs[g, h], NT)
            dp = dot(v_rows, gs[g, h], NT)
            one = inv[g, pl.ds(8 * h, 1), :]
            mean = row[g, pl.ds(8 * h, 1), :]
            low, dlow = [], []
            for jj in range(blocks):
                t, w = weights_of(cut(s, jj, tok), los[h], jj, jj == blocks - 1, tok)
                p = w * one
                low.append(p.astype(jnp.bfloat16))
                ds = p * slope(t) * (cut(dp, jj, tok) - mean)
                dlow.append(ds.astype(jnp.bfloat16))
            dvs.append(dot(jnp.concatenate(low[FAR - h :], 0), gs[g, h], NN))
            dks.append(dot(jnp.concatenate(dlow[FAR - h :], 0), qs[g, h], NN))
            dq_t = dot(k_rows.T, jnp.concatenate(dlow, 0), NN)
            dq_s[g, lax.bitwise_xor(core, h)] = dq_t.T.astype(jnp.bfloat16)
        spread(core, dvs, FAR, (dva, dvc), g, tok)
        spread(core, dks, FAR, (dka, dkc), g, tok)
        for r, dq in enumerate((dq0, dq1)):
            for hd in range(2):
                dq[:, lanes_at(2 * g + hd)] = dq_s[g, r, hd * tok : (hd + 1) * tok, :]
        return 0

    lax.fori_loop(0, groups, step, 0, unroll=True)


def merge(tok, groups, core_ref, mine, came, out):
    out[...] = (mine[...] + came[...].astype(jnp.float32)).astype(out.dtype)


def merge_halves(tok, groups, core_ref, mine, came, own, other):
    for r, out in enumerate((own, other)):
        rows = pl.ds(r * tok, tok)
        out[...] = (mine[rows, :] + came[rows, :].astype(jnp.float32)).astype(out.dtype)


def call(body, tok, groups, args, outs, scratch=()):
    vmem = pl.BlockSpec(memory_space=pltpu.VMEM)
    return pl.pallas_call(
        functools.partial(body, tok, groups),
        in_specs=[pl.BlockSpec(memory_space=pltpu.SMEM)] + [vmem] * (len(args) - 1),
        out_specs=[vmem] * len(outs),
        out_shape=[jax.ShapeDtypeStruct(s, d) for s, d in outs],
        scratch_shapes=list(scratch),
        compiler_params=pltpu.CompilerParams(vmem_limit_bytes=VMEM_LIMIT),
        name=body.__name__,
    )(*args)


VMEM_LIMIT = 16 * 1024 * 1024


def local(queries, keys, values, grad_out, segment):
    tok = queries.shape[0]
    kv_width = keys.shape[1]
    half = kv_width // 2
    groups = half // HEAD_DIM
    q_half = queries.shape[1] // 2
    bf16, f32 = jnp.bfloat16, jnp.float32
    core = lax.rem(lax.axis_index(AXES), 2)
    core_arr = core.reshape(1).astype(jnp.int32)

    def part(x, which, width):
        return lax.dynamic_slice(x, (0, which * width), (x.shape[0], width))

    k_in = swap(keys)
    seg_in = swap(segment)
    ids = jnp.concatenate([segment, seg_in]) + 1
    seg_rows = jnp.pad(ids.astype(bf16)[None, :], ((0, SEG_ROWS - 1), (0, half - 2 * tok)))
    kc = jnp.concatenate([part(keys, core, half), part(k_in, core, half), seg_rows], 0)
    v_in = swap(values)
    values, _ = lax.optimization_barrier((values, kc))
    vc = jnp.concatenate([part(values, core, half), part(v_in, core, half)], 0)
    ka = hop(kc, 1)
    va = hop(vc, 1)
    queries, grad_out, _ = lax.optimization_barrier((queries, grad_out, kc))
    qg_in = swap(jnp.concatenate([part(queries, 1 - core, q_half), part(grad_out, 1 - core, q_half)], 0))

    rows = ((groups, 2, 2 * tok, HEAD_DIM), bf16)
    stat = ((groups, 16, 2 * tok), f32)
    kv_f = ((2 * tok, half), f32)
    kv_b = ((2 * tok, half), bf16)
    dq_o = ((tok, q_half), bf16)

    qs, gs, lo = call(
        stack_heads, tok, groups, (core_arr, queries, grad_out, qg_in, kc),
        [rows, rows, ((8, tok), jnp.int32)])
    va, qs, gs, lo = lax.optimization_barrier((va, qs, gs, lo))
    wk = ahead(kc)
    wv = ahead(vc)
    kb = forward(ka)
    vb = forward(va)
    tot, term = call(
        near_sums, tok, groups, (core_arr, lo, qs, gs, ka, kc, va, vc), [stat, stat])
    dvb, inv = call(
        far_values, tok, groups, (core_arr, lo, qs, gs, ka, kb, wk, tot), [kv_b, stat])
    cv = hop(dvb, -1)
    dkb, row = call(
        far_keys, tok, groups, (core_arr, lo, qs, gs, ka, kb, wk, va, vb, wv, inv, term), [kv_b, stat])
    ck = hop(dkb, -1)
    dva, dvc, dka, dkc, dq0, dq1 = call(
        near_grads, tok, groups, (core_arr, lo, qs, gs, kb, wk, ka, kc, vb, wv, va, vc, inv, row),
        [kv_f, kv_f, kv_f, kv_f, dq_o, dq_o],
        [pltpu.VMEM((groups, 2, 2 * tok, HEAD_DIM), bf16)])
    (dv_out,) = call(merge, tok, groups, (core_arr, dva, cv), [kv_b])
    dv = hop(dv_out, -1)
    dk_own, dk_other = call(merge_halves, tok, groups, (core_arr, dka, ck), [((tok, half), bf16)] * 2)
    dkc, dq1, _ = lax.optimization_barrier((dkc, dq1, dv_out))
    dk_same = hop(dk_own, -1)
    dk_cross = cross(dk_other, -1)
    def place(mine, other):
        first = jnp.where(core == 0, mine, other)
        second = jnp.where(core == 0, other, mine)
        return jnp.concatenate([first, second], 1)

    grad_q = place(dq0, swap(dq1))
    sum_v = dvc + dv.astype(f32)
    grad_v = place(sum_v[:tok].astype(bf16), swap(sum_v[tok:].astype(bf16)))
    other_k = swap(dkc[tok:])
    dk_cross, grad_v = lax.optimization_barrier((dk_cross, grad_v))
    same = (dkc[:tok] + dk_same.astype(f32)).astype(bf16)
    other = (other_k + dk_cross.astype(f32)).astype(bf16)
    grad_k = place(same, other)
    return grad_q, grad_k, grad_v


def solution(mesh):
    rows = P(AXES, None)
    return jax.shard_map(
        local,
        mesh=mesh,
        in_specs=(rows, rows, rows, rows, P(AXES)),
        out_specs=(rows, rows, rows),
        check_vma=False,
    )
```
